128 devices in a mesh: section: 4 (over x), group: 4 (over y_hi, core), head: 8 (over z, y_lo).
Axes of the slice: x: 4, y: 4 (y_hi: 2, y_lo: 2; y = y_hi * 2 + y_lo), z: 4, core: 2. Of those that a mesh axis runs over, the one named last changes fastest.
Arguments:
- queries: bfloat16 [4, 8, 128, 576], P('group', None, ('section', 'head')), may hold values from -84 to 84
- cache: bfloat16 [4, 8, 4096, 576], P('group', None, ('section', 'head')), may hold values from -6 to 6
- kept_length: int32 [4, 8], P('group'), may hold values from 1024 to 4096, as said below
- w_uv: bfloat16 [128, 512, 128], P(('section', 'head')), may hold values from -0.75 to 0.75
- w_out: bfloat16 [16384, 7168], P(('section', 'head')), may hold values from -0.09375 to 0.09375
- resid: bfloat16 [4, 8, 7168], P('group', 'section', 'head'), may hold values from -3 to 3
- picks: int32 [4, 8, 8], P('group', 'section'), may hold values from 0 to 15, all different within a row; in each aligned block of 2 rows (0 to 1, 2 to 3, ..., all dimensions but the last counted through in order) at most 2 rows name the same one
- pick_logits: float32 [4, 8, 8], P('group', 'section'), may hold values from -6 to 6
- w_gate: bfloat16 [16, 7168, 2048], P(('section', 'group'), 'head'), may hold values from -0.0625 to 0.0625
- w_up: bfloat16 [16, 7168, 2048], P(('section', 'group'), 'head'), may hold values from -0.0625 to 0.0625
- w_down: bfloat16 [16, 2048, 7168], P(('section', 'group'), None, 'head'), may hold values from -0.125 to 0.125
Outputs:
- out: bfloat16 [4, 8, 7168], P('group', 'section', 'head')
The draws below stay inside these ranges and needn't reach their ends.
Inputs may be any that keep to these rules, and one draw needn't show every extreme that they name: Request j of group g keeps its first kept_length[g, j] positions; some request keeps all 4096. Each token picks 8 different experts; since each token's 8 picks differ, an expert receives at most 2 of the 2 tokens of one section index of a group.
All inputs are finite; a program needn't handle non-finite values.
Results may differ from the reference program's by a relative error of at most 0.012.
Values may be sent and summed in bfloat16 or wider, within the bound.
No kernel may reach another device: no remote copies, remote signals or barrier semaphores. Data moves between devices by JAX's collectives and lax.ppermute only.
A program may use at most 256 MiB of HBM per device.

```python
import math
import jax
import jax.numpy as jnp
import numpy as np
from jax import lax

LAT = 512
ROPE = 64
VDIM = 128
D = 7168
FF = 2048
TOPK = 8
KEEP = 4096
REQ_G = 8
HEADS = 128
GROUPS = 4
BLOCKS = 32
BLOCK_LEN = 128
ROWS_DEV = 2
EXPERTS = 16
CAP = 2


def anchor_rows(key):
    return jax.random.truncated_normal(key, -6.0, 6.0, (GROUPS, REQ_G, 2, LAT + ROPE), jnp.float32)


def draw_cache(key, part):
    anchors = anchor_rows(key)
    key = jax.random.fold_in(key, 11)
    key_one = jax.random.fold_in(key, 0)
    dims_all = (GROUPS, REQ_G, KEEP, LAT + ROPE)
    drawn_values = jax.random.truncated_normal(key_one, -6.0, 6.0, dims_all, jnp.float32)
    drawn_values = drawn_values.at[:, :, 0].set(anchors[:, :, 0])
    drawn_values = drawn_values.at[:, :, KEEP // 8].set(anchors[:, :, 1])
    return drawn_values.astype(jnp.bfloat16)


def draw_queries(key, part):
    key = jax.random.fold_in(key, 12)
    key_one = jax.random.fold_in(key, 0)
    dims_all = (GROUPS, REQ_G, HEADS, LAT + ROPE)
    drawn_values = jax.random.truncated_normal(key_one, -6.0, 6.0, dims_all, jnp.float32)
    return drawn_values.astype(jnp.bfloat16)


def draw_kept_length(key, part):
    key = jax.random.fold_in(key, 13)
    key_one, key_two = jax.random.split(key)
    drawn_values = jax.random.randint(key_one, (GROUPS, REQ_G), KEEP // 4, KEEP + 1, jnp.int32)
    target = jax.random.randint(key_two, (), 0, GROUPS * REQ_G, jnp.int32)
    flat_index = jnp.arange(GROUPS * REQ_G, dtype=jnp.int32).reshape(GROUPS, REQ_G)
    return jnp.where(flat_index == target, KEEP, drawn_values).astype(jnp.int32)


def strengthened(values, stream_key, source, target, blocks, factor):
    def block_of(axis_at):
        return (jnp.arange(values.shape[axis_at]) // (values.shape[axis_at] // blocks)).reshape((-1,) + (1,) * (values.ndim - 1 - axis_at))

    near = jax.random.permutation(stream_key, blocks)[block_of(target)]
    far = (block_of(target) + blocks // 2) % blocks
    return jnp.where((block_of(source) == near) | (block_of(source) == far), factor * values, values)


def block_scale(stream_key, shape, cuts, smallest, high):
    def one(dim, shards_of):
        heights = jax.random.uniform(jax.random.fold_in(jax.random.fold_in(stream_key, 6), dim), (shards_of,), jnp.float32, smallest / len(cuts), high / len(cuts))
        return jnp.repeat(jnp.exp(heights), shape[dim] // shards_of).reshape((-1,) + (1,) * (len(shape) - dim - 1))

    gain = one(*cuts[0])
    for cut in cuts[1:]:
        gain = gain * one(*cut)
    return gain


def deal_out(rng, own, number, rows, number_of, top, reach, lean):
    ranking = jax.random.permutation(rng, number_of)
    crowded, usual = portions_of(number_of, rows * top, reach, lean, True), portions_of(number_of, rows * top, reach, lean, False)
    places = jnp.arange(number_of)

    def named(lengths, turn):
        used = int((lengths > 0).sum())
        fixed = max(1, used // 4)
        shifted = fixed + (places - fixed + turn * (used - fixed)) % max(1, number_of - fixed)
        return jnp.zeros((number_of,), jnp.int32).at[ranking[jnp.where(places < fixed, places, shifted)]].set(jnp.asarray(lengths, jnp.int32))

    lengths = jnp.where(number % 4 == 0, named(crowded, number // 4), named(usual, number - number // 4 - 1))
    mixed = jax.random.permutation(jax.random.fold_in(own, 3), number_of)
    giver, sink = mixed[0:number_of // 2 * 2:2], mixed[1:number_of // 2 * 2:2]
    margin = jnp.minimum(lengths[giver] - 1, reach - lengths[sink]) // 2
    margin = jnp.where((giver == ranking[0]) | (sink == ranking[0]) | (lengths[sink] == 0), 0, jnp.maximum(margin, 0))
    shifted = jax.random.randint(jax.random.fold_in(own, 4), (number_of // 2,), 0, 1 << 20) % (margin + 1)
    lengths = lengths.at[giver].add(-shifted).at[sink].add(shifted)
    labels = jnp.searchsorted(jnp.cumsum(lengths), jnp.arange(rows * top), side="right").astype(jnp.int32)
    listing = labels.reshape(top, rows).T
    listing = listing[jax.random.permutation(jax.random.fold_in(own, 1), rows)]
    turn = jax.random.randint(jax.random.fold_in(own, 2), (rows, 1), 0, top)
    return jnp.take_along_axis(listing, (jnp.arange(top)[None, :] + turn) % top, axis=1)


def portions_of(amount, total, limit, slope, full):
    portions = [(1 << 20) // math.isqrt(grade ** slope) + 1 for grade in range(1, amount + 1)]
    largest = limit if full else min(limit, max(-(-total // amount), total * portions[0] // sum(portions)))
    least = 1 if total - largest >= amount - 1 else 0
    counts, rest = [largest] + [least] * (amount - 1), total - largest - least * (amount - 1)
    while rest > 0:
        free = [i for i in range(1, amount) if counts[i] < largest] or [i for i in range(1, amount) if counts[i] < limit]
        mass, remaining = sum([portions[i] for i in free]), rest
        for i in free:
            more = min(limit - counts[i], max(1, remaining * portions[i] // mass), rest)
            counts[i] = counts[i] + more
            rest = rest - more
    return np.array(counts)


def gaussian(stream_key, dims, spread, most, pieces=(), kind=jnp.bfloat16):
    loudness = block_scale(stream_key, dims, pieces, -0.22, 0.18) if pieces else 1.0
    entries = jax.random.normal(stream_key, dims, jnp.float32) * spread * loudness
    return jnp.minimum(jnp.maximum(entries, -most), most).astype(kind)


def heavy_noise(own_key, dims, deviation, limit, pieces, heavy, kind=jnp.bfloat16):
    drawn = deviation * jax.random.normal(own_key, dims, jnp.float32)
    if pieces:
        drawn = drawn * block_scale(own_key, dims, pieces, -0.22, 0.18)
    return jnp.clip(strengthened(drawn, jax.random.fold_in(own_key, 3), *heavy), -limit, limit).astype(kind)


def setup_inputs(seed: int = 0) -> dict:
    key_list = jax.random.split(jax.random.key(seed), 12)
    queries = draw_queries(jax.random.fold_in(key_list[11], 71), 0)
    cache = draw_cache(jax.random.fold_in(key_list[11], 71), 0)
    kept_length = draw_kept_length(jax.random.fold_in(key_list[11], 71), 0)
    w_uv = gaussian(key_list[3], (HEADS, LAT, VDIM), (LAT // 9) ** -0.5, 0.75, ((0, 32),))
    w_out = heavy_noise(key_list[4], (HEADS * VDIM, D), (HEADS * VDIM) ** -0.5, 0.09375, ((0, 32),), (0, 1, 32, 2.75))
    resid = gaussian(key_list[5], (GROUPS, REQ_G, D), 0.5, 3.0, ((0, 4), (1, 4), (2, 8)))
    picks_keys = jax.random.split(jax.random.fold_in(key_list[6], 1), GROUPS * REQ_G // ROWS_DEV)
    picks_turns = jax.random.permutation(jax.random.fold_in(key_list[6], 3), GROUPS * REQ_G // ROWS_DEV)
    picks = jax.vmap(lambda own, number: deal_out(jax.random.fold_in(key_list[6], 2), own, number, ROWS_DEV, EXPERTS, TOPK, CAP, 2))(picks_keys, picks_turns).reshape((GROUPS, REQ_G, TOPK))
    pick_logits = gaussian(key_list[7], (GROUPS, REQ_G, TOPK), 1.5, 6.0, ((0, 4), (1, 4)), jnp.float32)
    w_gate = gaussian(key_list[8], (EXPERTS, D, FF), D ** -0.5, 0.0625, ((0, 16), (1, 8)))
    w_up = gaussian(key_list[9], (EXPERTS, D, FF), D ** -0.5, 0.0625, ((0, 16), (1, 8)))
    w_down = gaussian(key_list[10], (EXPERTS, FF, D), FF ** -0.5, 0.125, ((0, 16), (2, 8)))
    return dict(queries=queries, cache=cache, kept_length=kept_length, w_uv=w_uv, w_out=w_out, resid=resid, picks=picks, pick_logits=pick_logits, w_gate=w_gate, w_up=w_up, w_down=w_down)


neg_fill = -1e+30
norm_eps = 1e-06
route_scale = 2.5

def reference(queries, cache, kept_length, w_uv, w_out, resid, picks, pick_logits, w_gate, w_up, w_down):
    score_scale = (VDIM + ROPE) ** (-0.5)

    def attend(operands):
        query_rows, cache_rows, length_rows = operands
        page_rows = cache_rows.reshape(REQ_G, BLOCKS, BLOCK_LEN, LAT + ROPE).astype(jnp.float32)
        scores = jnp.einsum('jnd,jbtd->jbnt', query_rows.astype(jnp.float32), page_rows) * score_scale
        position = jnp.arange(BLOCKS, dtype=jnp.int32)[:, None] * BLOCK_LEN + jnp.arange(BLOCK_LEN, dtype=jnp.int32)[None, :]
        counted = position[None, :, None, :] < length_rows[:, None, None, None]
        masked = jnp.where(counted, scores, neg_fill)
        block_max = lax.optimization_barrier(jnp.max(masked, axis=-1))
        weights = jnp.where(counted, jnp.exp(masked - block_max[..., None]), 0.0)
        block_sum = lax.optimization_barrier(jnp.sum(weights, axis=-1))
        rounded = lax.optimization_barrier(weights.astype(jnp.bfloat16)).astype(jnp.float32)
        block_out = jnp.einsum('jbnt,jbtl->jbnl', rounded, page_rows[..., :LAT])
        row_max = lax.optimization_barrier(jnp.max(block_max, axis=1, keepdims=True))
        factor = jnp.exp(block_max - row_max)
        total = lax.optimization_barrier(jnp.sum(factor * block_sum, axis=1))
        latent = (lax.optimization_barrier(jnp.sum(factor[..., None] * block_out, axis=1)) / total[..., None]).astype(jnp.bfloat16)
        values = jnp.einsum('jnl,nlv->jnv', latent.astype(jnp.float32), w_uv.astype(jnp.float32)).astype(jnp.bfloat16)
        return jnp.dot(values.reshape(REQ_G, HEADS * VDIM), w_out, preferred_element_type=jnp.float32)
    attended = lax.map(attend, (queries, cache, kept_length))
    hidden = (resid.astype(jnp.float32) + attended).astype(jnp.bfloat16)
    token_rows = hidden.reshape(GROUPS * REQ_G, D)
    scale_rows = lax.rsqrt(lax.optimization_barrier(jnp.mean(jnp.square(token_rows.astype(jnp.float32)), axis=-1, keepdims=True)) + norm_eps)

    def expert(matrices):
        gate_mat, up_mat, down_mat = matrices
        gate_part = jnp.dot(token_rows, gate_mat, preferred_element_type=jnp.float32) * scale_rows
        up_part = jnp.dot(token_rows, up_mat, preferred_element_type=jnp.float32) * scale_rows
        active = (jax.nn.silu(gate_part) * up_part).astype(jnp.bfloat16)
        return jnp.dot(active, down_mat, preferred_element_type=jnp.float32).astype(jnp.bfloat16)
    outputs = lax.map(expert, (w_gate, w_up, w_down))
    chosen = picks.reshape(GROUPS * REQ_G, TOPK)
    affinity = jax.nn.sigmoid(pick_logits.reshape(GROUPS * REQ_G, TOPK))
    pick_share = route_scale * affinity / lax.optimization_barrier(jnp.sum(affinity, axis=-1, keepdims=True))
    row_ids = jnp.arange(GROUPS * REQ_G, dtype=jnp.int32)
    picked = outputs[chosen, row_ids[:, None]]
    mixture = lax.optimization_barrier(jnp.sum(pick_share[..., None] * picked.astype(jnp.float32), axis=1))
    return (token_rows.astype(jnp.float32) + mixture).astype(jnp.bfloat16).reshape(GROUPS, REQ_G, D)
```

```python
import jax
import jax.numpy as jnp
from jax import lax
from jax.sharding import PartitionSpec as P

LAT = 512
ROPE = 64
VDIM = 128
D = 7168

neg_fill = -1e30
norm_eps = 1e-06
route_scale = 2.5
f32 = jnp.float32
bf16 = jnp.bfloat16


def exchange(x, axes):
    return lax.all_to_all(x, axes, split_axis=0, concat_axis=0, tiled=True)


def parts_of(x):
    high = lax.reduce_precision(x, 8, 7)
    rest = x - high
    middle = lax.reduce_precision(rest, 8, 7)
    return high.astype(bf16), middle.astype(bf16), (rest - middle).astype(bf16)


def local(
    queries, cache, kept_length, w_uv, w_out, resid, picks, pick_logits, w_gate, w_up, w_down
):
    n_section = lax.axis_size("section")
    n_group = lax.axis_size("group")
    n_head = lax.axis_size("head")
    n_shard = n_section * n_head
    n_expert = n_section * n_group
    section = lax.axis_index("section")
    group = lax.axis_index("group")
    head = lax.axis_index("head")
    reqs, heads_dev, width = queries.shape[1:]
    block_len = cache.shape[2]
    rows_dev, width_dev = resid.shape[1:]

    spread = jnp.broadcast_to(queries[0][None], (n_section, reqs, heads_dev, width))
    q_all = exchange(spread.reshape(n_shard, heads_dev, width), ("section", "head"))
    q_all = q_all.reshape(n_shard * heads_dev, width)
    pages = exchange(jnp.swapaxes(cache[0], 1, 2), "head")

    scores = jnp.einsum("nd,bdt->nbt", q_all, pages, preferred_element_type=f32) * (
        (VDIM + ROPE) ** -0.5
    )
    position = (section * n_head * block_len) + jnp.arange(n_head * block_len, dtype=jnp.int32)
    length = lax.dynamic_index_in_dim(kept_length[0], head, 0, keepdims=False)
    counted = (position < length).reshape(1, n_head, block_len)
    masked = jnp.where(counted, scores, neg_fill)
    top = jnp.max(masked, axis=(1, 2), keepdims=True)
    weights = jnp.where(counted, jnp.exp(masked - top), 0.0)
    total = jnp.sum(weights, axis=(1, 2))
    part_out = jnp.einsum(
        "nbt,blt->nl", weights.astype(bf16), pages[:, :LAT], preferred_element_type=f32
    )
    any_kept = total > 0
    safe = jnp.where(any_kept, total, 1.0)
    part_out = (part_out / safe[:, None]).astype(bf16)
    level = jnp.where(any_kept, top[:, 0, 0] + jnp.log(safe), neg_fill)
    extra = jnp.stack(parts_of(level), axis=-1)
    extra = jnp.pad(extra, ((0, 0), (0, 125)))
    sent = jnp.concatenate([part_out, extra], axis=1).reshape(n_shard, heads_dev, LAT + 128)
    got = exchange(sent, ("section", "head")).reshape(n_section, reqs, heads_dev, LAT + 128)
    levels = jnp.sum(got[..., LAT : LAT + 3].astype(f32), axis=-1)
    share = jnp.exp(levels - jnp.max(levels, axis=0))
    share = share / jnp.sum(share, axis=0)
    latent = jnp.sum(share[..., None] * got[..., :LAT].astype(f32), axis=0).astype(bf16)

    values = jnp.einsum("jnl,nlv->jnv", latent, w_uv, preferred_element_type=f32).astype(bf16)
    values = values.reshape(reqs, heads_dev * VDIM)
    term = jnp.dot(values, w_out, preferred_element_type=f32).astype(bf16)
    term = jnp.swapaxes(term.reshape(reqs, n_head, width_dev), 0, 1)
    term = jnp.sum(exchange(term, "head").astype(f32), axis=0)
    own = (jnp.arange(reqs) // rows_dev == section)[:, None]
    term = term + jnp.where(own, jnp.tile(resid[0].astype(f32), (n_section, 1)), 0.0)
    term = jnp.broadcast_to(term.astype(bf16)[None], (n_expert, reqs, width_dev))
    terms = exchange(term, ("section", "group")).reshape(n_section, n_group, reqs, width_dev)
    hidden = jnp.sum(terms.astype(f32), axis=0).astype(bf16)
    rows = hidden.reshape(n_group * reqs, width_dev)

    gate = jnp.dot(rows, w_gate[0], preferred_element_type=f32).astype(bf16)
    up = jnp.dot(rows, w_up[0], preferred_element_type=f32).astype(bf16)
    squares = jnp.sum(jnp.square(rows.astype(f32)), axis=-1)
    extra = jnp.pad(jnp.stack(parts_of(squares), axis=-1), ((0, 0), (0, 125)))
    count = rows.shape[0]
    ff_dev = gate.shape[1] // n_head
    both = jnp.concatenate(
        [
            gate.reshape(count, n_head, ff_dev),
            up.reshape(count, n_head, ff_dev),
            jnp.broadcast_to(extra[:, None], (count, n_head, 128)),
        ],
        axis=-1,
    )
    both = jnp.sum(exchange(jnp.swapaxes(both, 0, 1), "head").astype(f32), axis=0)
    squares = jnp.sum(both[:, 2 * ff_dev : 2 * ff_dev + 3], axis=-1, keepdims=True)
    factor = lax.rsqrt(squares / D + norm_eps)
    act = jax.nn.silu(both[:, :ff_dev] * factor) * (both[:, ff_dev : 2 * ff_dev] * factor)
    act = jnp.broadcast_to(act.astype(bf16)[None], (n_head, count, ff_dev))
    act = jnp.swapaxes(exchange(act, "head"), 0, 1).reshape(count, n_head * ff_dev)
    served = jnp.dot(act, w_down[0], preferred_element_type=f32).astype(bf16)
    served = served.reshape(n_group, n_section, rows_dev, width_dev)
    served = jnp.swapaxes(served, 0, 1).reshape(n_expert, rows_dev, width_dev)
    back = exchange(served, ("section", "group"))

    affinity = jax.nn.sigmoid(pick_logits[0])
    pick_share = route_scale * affinity / jnp.sum(affinity, axis=-1, keepdims=True)
    named = picks[0][..., None] == jnp.arange(n_expert, dtype=jnp.int32)
    weight = jnp.sum(jnp.where(named, pick_share[..., None], 0.0), axis=1)
    mixture = jnp.sum(weight.T[..., None] * back.astype(f32), axis=0)
    mine = lax.dynamic_slice(
        rows, (group * reqs + section * rows_dev, 0), (rows_dev, width_dev)
    )
    return (mine.astype(f32) + mixture).astype(bf16)[None]


def solution(mesh):
    return jax.shard_map(
        local,
        mesh=mesh,
        in_specs=(
            P("group", None, ("section", "head"), None),
            P("group", None, ("section", "head"), None),
            P("group", None),
            P(("section", "head"), None, None),
            P(("section", "head"), None),
            P("group", "section", "head"),
            P("group", "section", None),
            P("group", "section", None),
            P(("section", "group"), "head", None),
            P(("section", "group"), "head", None),
            P(("section", "group"), None, "head"),
        ),
        out_specs=P("group", "section", "head"),
        check_vma=False,
    )
```

```python
import functools

import jax
import jax.numpy as jnp
from jax import lax
from jax.experimental import pallas as pl
from jax.experimental.pallas import tpu as pltpu
from jax.sharding import PartitionSpec as P

LAT = 512
ROPE = 64
VDIM = 128
D = 7168

neg_fill = -1e30
norm_eps = 1e-06
route_scale = 2.5
f32 = jnp.float32
bf16 = jnp.bfloat16
SPLIT = ("section", "head")
VMEM = pl.BlockSpec(memory_space=pltpu.VMEM)
SMEM = pl.BlockSpec(memory_space=pltpu.SMEM)
LIMIT = 48 * 1024 * 1024


def exchange(x, axes):
    return lax.all_to_all(x, axes, split_axis=0, concat_axis=0, tiled=True)


def contract(a, b, dims):
    return lax.dot_general(a, b, (dims, ((), ())), preferred_element_type=f32)


def in_lanes(x):
    high = x.astype(bf16).astype(f32)
    rest = x - high
    middle = rest.astype(bf16).astype(f32)
    lane = lax.broadcasted_iota(jnp.int32, (x.shape[0], 128), 1)
    zero = jnp.zeros((x.shape[0], 128), f32)
    low = jnp.where(lane == 2, rest - middle, zero)
    return jnp.where(lane == 0, high, jnp.where(lane == 1, middle, low))


def attend_kernel(n_section, n_head, length_ref, q_ref, k0, k1, k2, k3, out_ref):
    section = lax.axis_index("section")
    head = lax.axis_index("head")
    label = 2 * (section % 2) + (head // 2) % 2
    block = k0.shape[2]
    sources = (
        (section, head),
        ((section + n_section - 1) % n_section, head),
        (section, (head + n_head - 2) % n_head),
        ((section + 1) % n_section, (head + 2) % n_head),
    )
    rows = q_ref.shape[0]
    first = lax.broadcasted_iota(jnp.int32, (rows, 1), 0) % 8 < 4
    limit = jnp.where(first, length_ref[0, 2 * label], length_ref[0, 2 * label + 1])
    lane = lax.broadcasted_iota(jnp.int32, (1, block), 1)
    position = jnp.concatenate([(s * n_head + h) * block + lane for s, h in sources], axis=1)
    pages = [jnp.concatenate([k[r] for k in (k0, k1, k2, k3)], axis=1) for r in range(2)]
    q = q_ref[...]
    scores = [contract(q, page, ((1,), (0,))) for page in pages]
    scores = jnp.where(first, scores[0], scores[1]) * ((VDIM + ROPE) ** -0.5)
    counted = position < limit
    top = jnp.max(jnp.where(counted, scores, neg_fill), axis=1, keepdims=True)
    weights = jnp.where(counted, jnp.exp(scores - top), 0.0)
    total = jnp.sum(weights, axis=1, keepdims=True)
    weights = weights.astype(bf16)
    outs = [contract(weights, page[:LAT], ((1,), (1,))) for page in pages]
    any_kept = total > 0
    safe = jnp.where(any_kept, total, 1.0)
    out_ref[:, :LAT] = (jnp.where(first, outs[0], outs[1]) / safe).astype(bf16)
    level = jnp.where(any_kept, top + jnp.log(safe), neg_fill)
    out_ref[:, LAT:] = in_lanes(level).astype(bf16)


def project_kernel(n_section, n_head, got_ref, uv_ref, out_w_ref, resid_ref, term_ref, values):
    step = pl.program_id(0)
    reqs = term_ref.shape[2]

    @pl.when(step == 0)
    def _():
        got = got_ref[...].astype(f32).reshape(n_section * n_head, 8, LAT + 128)
        level = jnp.sum(got[:, :, LAT:], axis=2, keepdims=True)
        merged = []
        for label in range(4):
            parts = [
                (2 * a + label // 2) * n_head + 2 * (2 * b + label % 2) + c
                for a in range(n_section // 2)
                for b in range(n_head // 4)
                for c in range(2)
            ]
            top = functools.reduce(jnp.maximum, [level[d] for d in parts])
            share = [jnp.exp(level[d] - top) for d in parts]
            total = functools.reduce(jnp.add, share)
            mix = functools.reduce(
                jnp.add, [w * got[d, :, :LAT] for w, d in zip(share, parts)]
            )
            merged.append(mix / total)
        latent = jnp.concatenate(merged, axis=0).astype(bf16)
        heads = uv_ref.shape[0]
        row = lax.broadcasted_iota(jnp.int32, (reqs, reqs * heads), 0)
        column = lax.broadcasted_iota(jnp.int32, (reqs, reqs * heads), 1)
        for i in range(heads):
            pick = (column == heads * row + i).astype(f32).astype(bf16)
            own = contract(pick, latent, ((1,), (0,))).astype(bf16)
            values[:, VDIM * i : VDIM * (i + 1)] = contract(own, uv_ref[i], ((1,), (0,)))

    term = contract(values[...].astype(bf16), out_w_ref[...], ((1,), (0,)))
    row = lax.broadcasted_iota(jnp.int32, term.shape, 0)
    resid = resid_ref[0].astype(f32)
    spread = jnp.where(row % 2 == 0, resid[0:1], resid[1:2])
    mine = (row // 2 == lax.axis_index("section")) & (step == lax.axis_index("head"))
    term = (term + jnp.where(mine, spread, 0.0)).astype(bf16)
    for s in range(n_section):
        term_ref[s, 0] = term


def expert_in_kernel(rows_ref, gate_ref, up_ref, both_ref):
    rows = rows_ref[...]
    ff = gate_ref.shape[2]
    both_ref[0, :, :ff] = contract(rows, gate_ref[0], ((1,), (0,))).astype(bf16)
    both_ref[0, :, ff : 2 * ff] = contract(rows, up_ref[0], ((1,), (0,))).astype(bf16)
    wide = rows.astype(f32)
    squares = jnp.sum(wide * wide, axis=1, keepdims=True)
    both_ref[0, :, 2 * ff :] = in_lanes(squares).astype(bf16)


def act_kernel(both_ref, act_ref):
    both = jnp.sum(both_ref[...].astype(f32), axis=0)
    ff = act_ref.shape[2]
    squares = jnp.sum(both[:, 2 * ff :], axis=1, keepdims=True)
    factor = lax.rsqrt(squares / D + norm_eps)
    gate = both[:, :ff] * factor
    act = gate * jax.nn.sigmoid(gate) * (both[:, ff : 2 * ff] * factor)
    act = act.astype(bf16)
    for k in range(act_ref.shape[0]):
        act_ref[k] = act


def expert_out_kernel(act_ref, down_ref, served_ref, total):
    step = pl.program_id(0)
    part = contract(act_ref[0], down_ref[0], ((1,), (0,)))

    @pl.when(step == 0)
    def _():
        total[...] = part

    @pl.when(step > 0)
    def _():
        total[...] += part

    @pl.when(step == pl.num_programs(0) - 1)
    def _():
        served_ref[...] = total[...].astype(bf16)


def params():
    return pltpu.CompilerParams(vmem_limit_bytes=LIMIT)


def local(
    queries, cache, kept_length, w_uv, w_out, resid, picks, pick_logits, w_gate, w_up, w_down
):
    n_section = lax.axis_size("section")
    n_group = lax.axis_size("group")
    n_head = lax.axis_size("head")
    n_shard = n_section * n_head
    n_expert = n_section * n_group
    section = lax.axis_index("section")
    group = lax.axis_index("group")
    head = lax.axis_index("head")
    reqs, heads_dev, width = queries.shape[1:]
    rows_dev, width_dev = resid.shape[1:]

    label = 2 * (section % 2) + (head // 2) % 2
    pages = jnp.swapaxes(cache[0], 1, 2).reshape(4, 2, width, cache.shape[2])

    def of_label(which):
        return lax.dynamic_index_in_dim(pages, which, 0, keepdims=False)

    def passed(which, ds, dz):
        pairs = [
            (
                s * n_head + h,
                (s + ds) % n_section * n_head + (h + 2 * dz) % n_head,
            )
            for s in range(n_section)
            for h in range(n_head)
        ]
        return lax.ppermute(of_label(which), SPLIT, pairs)

    moved = [passed(label ^ 2, 1, 0), passed(label ^ 1, 0, 1), passed(label ^ 3, -1, -1)]
    spread = queries[0].reshape(1, 2, 1, 2, 1, 2 * heads_dev, width)
    spread = jnp.broadcast_to(
        spread, (n_section // 2, 2, n_head // 4, 2, 2, 2 * heads_dev, width)
    )
    q_all = exchange(spread.reshape(n_shard * 2 * heads_dev, width), SPLIT)
    sent = pl.pallas_call(
        functools.partial(attend_kernel, n_section, n_head),
        out_shape=jax.ShapeDtypeStruct((q_all.shape[0], LAT + 128), bf16),
        in_specs=[SMEM] + [VMEM] * 5,
        out_specs=VMEM,
        compiler_params=params(),
    )(kept_length, q_all, of_label(label), *moved)
    got = exchange(sent, SPLIT)

    term = pl.pallas_call(
        functools.partial(project_kernel, n_section, n_head),
        out_shape=jax.ShapeDtypeStruct((n_section, n_head, reqs, width_dev), bf16),
        grid=(n_head,),
        in_specs=[
            pl.BlockSpec(got.shape, lambda k: (0, 0)),
            pl.BlockSpec(w_uv.shape, lambda k: (0, 0, 0)),
            pl.BlockSpec((w_out.shape[0], width_dev), lambda k: (0, k)),
            pl.BlockSpec(resid.shape, lambda k: (0, 0, 0)),
        ],
        out_specs=pl.BlockSpec((n_section, 1, reqs, width_dev), lambda k: (0, k, 0, 0)),
        scratch_shapes=[pltpu.VMEM((reqs, heads_dev * VDIM), f32)],
        compiler_params=params(),
    )(got, w_uv, w_out, resid)
    terms = exchange(term.reshape(n_shard * reqs, width_dev), SPLIT)
    hidden = jnp.sum(terms.reshape(n_shard, reqs, width_dev).astype(f32), axis=0).astype(bf16)

    def from_group(d):
        return lax.ppermute(hidden, "group", [(g, g ^ d) for g in range(n_group)])

    others = [hidden] + [from_group(d) for d in range(1, n_group)]
    rows = jnp.concatenate(others, axis=0)

    ff_dev = w_gate.shape[2] // n_head
    count = rows.shape[0]
    both = pl.pallas_call(
        expert_in_kernel,
        out_shape=jax.ShapeDtypeStruct((n_head, count, 2 * ff_dev + 128), bf16),
        grid=(n_head,),
        in_specs=[
            pl.BlockSpec(rows.shape, lambda k: (0, 0)),
            pl.BlockSpec((1, width_dev, ff_dev), lambda k: (0, 0, k)),
            pl.BlockSpec((1, width_dev, ff_dev), lambda k: (0, 0, k)),
        ],
        out_specs=pl.BlockSpec((1, count, 2 * ff_dev + 128), lambda k: (k, 0, 0)),
        compiler_params=params(),
    )(rows, w_gate, w_up)
    both = exchange(both, "head")
    act = pl.pallas_call(
        act_kernel,
        out_shape=jax.ShapeDtypeStruct((n_head, count, ff_dev), bf16),
        in_specs=[VMEM],
        out_specs=VMEM,
        compiler_params=params(),
    )(both)
    act = exchange(act, "head")
    served = pl.pallas_call(
        expert_out_kernel,
        out_shape=jax.ShapeDtypeStruct((count, width_dev), bf16),
        grid=(n_head,),
        in_specs=[
            pl.BlockSpec((1, count, ff_dev), lambda k: (k, 0, 0)),
            pl.BlockSpec((1, ff_dev, width_dev), lambda k: (0, k, 0)),
        ],
        out_specs=pl.BlockSpec((count, width_dev), lambda k: (0, 0)),
        scratch_shapes=[pltpu.VMEM((count, width_dev), f32)],
        compiler_params=params(),
    )(act, w_down)
    served = served.reshape(n_group, n_section, rows_dev, width_dev)
    served = jnp.swapaxes(served, 0, 1)
    order = jnp.arange(n_group, dtype=jnp.int32) ^ group
    served = jnp.take(served, order, axis=1).reshape(n_expert, rows_dev, width_dev)
    back = exchange(served, ("section", "group"))

    affinity = jax.nn.sigmoid(pick_logits[0])
    pick_share = route_scale * affinity / jnp.sum(affinity, axis=-1, keepdims=True)
    named = picks[0][..., None] == jnp.arange(n_expert, dtype=jnp.int32)
    weight = jnp.sum(jnp.where(named, pick_share[..., None], 0.0), axis=1)
    mixture = jnp.sum(weight.T[..., None] * back.astype(f32), axis=0)
    mine = lax.dynamic_slice(hidden, (section * rows_dev, 0), (rows_dev, width_dev))
    return (mine.astype(f32) + mixture).astype(bf16)[None]


def solution(mesh):
    return jax.shard_map(
        local,
        mesh=mesh,
        in_specs=(
            P("group", None, ("section", "head"), None),
            P("group", None, ("section", "head"), None),
            P("group", None),
            P(("section", "head"), None, None),
            P(("section", "head"), None),
            P("group", "section", "head"),
            P("group", "section", None),
            P("group", "section", None),
            P(("section", "group"), "head", None),
            P(("section", "group"), "head", None),
            P(("section", "group"), None, "head"),
        ),
        out_specs=P("group", "section", "head"),
        check_vma=False,
    )
```

```python
import functools

import jax
import jax.numpy as jnp
from jax import lax
from jax.experimental import pallas as pl
from jax.experimental.pallas import tpu as pltpu
from jax.sharding import PartitionSpec as P

LAT = 512
ROPE = 64
VDIM = 128
D = 7168

neg_fill = -1e30
norm_eps = 1e-06
route_scale = 2.5
f32 = jnp.float32
bf16 = jnp.bfloat16
SPLIT = ("section", "head")
VMEM = pl.BlockSpec(memory_space=pltpu.VMEM)
SMEM = pl.BlockSpec(memory_space=pltpu.SMEM)


def exchange(x, axes):
    return lax.all_to_all(x, axes, split_axis=0, concat_axis=0, tiled=True)


def contract(a, b, dims):
    return lax.dot_general(a, b, (dims, ((), ())), preferred_element_type=f32)


def in_lanes(x):
    high = x.astype(bf16).astype(f32)
    rest = x - high
    middle = rest.astype(bf16).astype(f32)
    lane = lax.broadcasted_iota(jnp.int32, (x.shape[0], 128), 1)
    zero = jnp.zeros((x.shape[0], 128), f32)
    low = jnp.where(lane == 2, rest - middle, zero)
    return jnp.where(lane == 0, high, jnp.where(lane == 1, middle, low))


def attend_kernel(n_section, n_head, length_ref, q_ref, k0, k1, k2, k3, out_ref):
    section = lax.axis_index("section")
    head = lax.axis_index("head")
    label = 2 * (section % 2) + (head // 2) % 2
    block = k0.shape[2]
    sources = (
        (section, head),
        ((section + n_section - 1) % n_section, head),
        (section, (head + n_head - 2) % n_head),
        ((section + 1) % n_section, (head + 2) % n_head),
    )
    rows = q_ref.shape[0]
    first = lax.broadcasted_iota(jnp.int32, (rows, 1), 0) % 8 < 4
    limit = jnp.where(first, length_ref[0, 2 * label], length_ref[0, 2 * label + 1])
    lane = lax.broadcasted_iota(jnp.int32, (1, block), 1)
    position = jnp.concatenate([(s * n_head + h) * block + lane for s, h in sources], axis=1)
    pages = [jnp.concatenate([k[r] for k in (k0, k1, k2, k3)], axis=1) for r in range(2)]
    q = q_ref[...]
    scores = [contract(q, page, ((1,), (0,))) for page in pages]
    scores = jnp.where(first, scores[0], scores[1]) * ((VDIM + ROPE) ** -0.5)
    counted = position < limit
    top = jnp.max(jnp.where(counted, scores, neg_fill), axis=1, keepdims=True)
    weights = jnp.where(counted, jnp.exp(scores - top), 0.0)
    total = jnp.sum(weights, axis=1, keepdims=True)
    weights = weights.astype(bf16)
    outs = [contract(weights, page[:LAT], ((1,), (1,))) for page in pages]
    any_kept = total > 0
    safe = jnp.where(any_kept, total, 1.0)
    out_ref[:, :LAT] = (jnp.where(first, outs[0], outs[1]) / safe).astype(bf16)
    level = jnp.where(any_kept, top + jnp.log(safe), neg_fill)
    out_ref[:, LAT:] = in_lanes(level).astype(bf16)


def project_kernel(n_section, n_head, got_ref, uv_ref, out_w_ref, resid_ref, term_ref):
    reqs, width_dev = term_ref.shape[2:]
    got = got_ref[...].astype(f32).reshape(n_section * n_head, 8, LAT + 128)
    level = jnp.sum(got[:, :, LAT:], axis=2, keepdims=True)
    merged = []
    for label in range(4):
        parts = [
            (2 * a + label // 2) * n_head + 2 * (2 * b + label % 2) + c
            for a in range(n_section // 2)
            for b in range(n_head // 4)
            for c in range(2)
        ]
        top = functools.reduce(jnp.maximum, [level[d] for d in parts])
        share = [jnp.exp(level[d] - top) for d in parts]
        total = functools.reduce(jnp.add, share)
        mix = functools.reduce(jnp.add, [w * got[d, :, :LAT] for w, d in zip(share, parts)])
        merged.append(mix / total)
    latent = jnp.concatenate(merged, axis=0).astype(bf16)
    heads = uv_ref.shape[0]
    row = lax.broadcasted_iota(jnp.int32, (reqs, reqs * heads), 0)
    column = lax.broadcasted_iota(jnp.int32, (reqs, reqs * heads), 1)
    values = []
    for i in range(heads):
        pick = (column == heads * row + i).astype(f32).astype(bf16)
        own = contract(pick, latent, ((1,), (0,))).astype(bf16)
        values.append(contract(own, uv_ref[i], ((1,), (0,))))
    values = jnp.concatenate(values, axis=1).astype(bf16)
    row = lax.broadcasted_iota(jnp.int32, (reqs, width_dev), 0)
    resid = resid_ref[0].astype(f32)
    spread = jnp.where(row % 2 == 0, resid[0:1], resid[1:2])
    spread = jnp.where(row // 2 == lax.axis_index("section"), spread, 0.0)
    head = lax.axis_index("head")
    for k in range(n_head):
        columns = slice(k * width_dev, (k + 1) * width_dev)
        term = contract(values, out_w_ref[:, columns], ((1,), (0,)))
        term = (term + jnp.where(head == k, spread, 0.0)).astype(bf16)
        for s in range(n_section):
            term_ref[s, k] = term


def expert_in_kernel(r0, r1, r2, r3, gate_ref, up_ref, both_ref):
    wide = jnp.concatenate([r[...].astype(f32) for r in (r0, r1, r2, r3)], axis=0)
    rows = wide.astype(bf16)
    squares = in_lanes(jnp.sum(wide * wide, axis=1, keepdims=True)).astype(bf16)
    n_head = both_ref.shape[0]
    ff = gate_ref.shape[2] // n_head
    for k in range(n_head):
        columns = slice(k * ff, (k + 1) * ff)
        both_ref[k, :, :ff] = contract(rows, gate_ref[0, :, columns], ((1,), (0,))).astype(bf16)
        both_ref[k, :, ff : 2 * ff] = contract(
            rows, up_ref[0, :, columns], ((1,), (0,))
        ).astype(bf16)
        both_ref[k, :, 2 * ff :] = squares


def act_kernel(both_ref, act_ref):
    both = jnp.sum(both_ref[...].astype(f32), axis=0)
    ff = act_ref.shape[2]
    squares = jnp.sum(both[:, 2 * ff :], axis=1, keepdims=True)
    factor = lax.rsqrt(squares / D + norm_eps)
    gate = both[:, :ff] * factor
    act = gate * jax.nn.sigmoid(gate) * (both[:, ff : 2 * ff] * factor)
    act = act.astype(bf16)
    for k in range(act_ref.shape[0]):
        act_ref[k] = act


def expert_out_kernel(n_section, n_group, act_ref, down_ref, served_ref):
    n_head, _, ff = act_ref.shape
    act = jnp.concatenate([act_ref[k] for k in range(n_head)], axis=1)
    total = contract(act, down_ref[0], ((1,), (0,)))
    group = lax.axis_index("group")
    rows_dev = served_ref.shape[1]
    for d in range(n_group):
        for s in range(n_section):
            start = (d * n_section + s) * rows_dev
            served_ref[s * n_group + (group ^ d)] = total[start : start + rows_dev].astype(bf16)


def finish_kernel(back_ref, picks_ref, logits_ref, hidden_ref, out_ref):
    n_expert, rows_dev, width_dev = back_ref.shape
    affinity = jax.nn.sigmoid(logits_ref[0])
    share = route_scale * affinity / jnp.sum(affinity, axis=1, keepdims=True)
    expert = lax.broadcasted_iota(jnp.int32, (rows_dev, n_expert), 1)
    weight = jnp.zeros((rows_dev, n_expert), f32)
    picks = picks_ref[0]
    for k in range(picks.shape[1]):
        weight += jnp.where(picks[:, k : k + 1] == expert, share[:, k : k + 1], 0.0)
    hidden = hidden_ref[...].astype(f32)
    section = lax.axis_index("section")
    total = jnp.zeros((rows_dev, width_dev), f32)
    for s in range(hidden.shape[0] // rows_dev):
        total += jnp.where(section == s, hidden[s * rows_dev : (s + 1) * rows_dev], 0.0)
    mixture = jnp.zeros((rows_dev, width_dev), f32)
    for e in range(n_expert):
        mixture += weight[:, e : e + 1] * back_ref[e].astype(f32)
    out_ref[0] = (total + mixture).astype(bf16)


def run(kernel, out_shape, *args, limit=16, cost=0):
    return pl.pallas_call(
        kernel,
        out_shape=jax.ShapeDtypeStruct(out_shape, bf16),
        in_specs=[SMEM if a.dtype == jnp.int32 and a.ndim == 2 else VMEM for a in args],
        out_specs=VMEM,
        compiler_params=pltpu.CompilerParams(vmem_limit_bytes=limit * 1024 * 1024),
        cost_estimate=pl.CostEstimate(
            flops=0, transcendentals=0, bytes_accessed=cost * 1024 * 1024
        )
        if cost
        else None,
    )(*args)


def local(
    queries, cache, kept_length, w_uv, w_out, resid, picks, pick_logits, w_gate, w_up, w_down
):
    n_section = lax.axis_size("section")
    n_group = lax.axis_size("group")
    n_head = lax.axis_size("head")
    n_shard = n_section * n_head
    n_expert = n_section * n_group
    section = lax.axis_index("section")
    head = lax.axis_index("head")
    reqs, heads_dev, width = queries.shape[1:]
    rows_dev, width_dev = resid.shape[1:]

    label = 2 * (section % 2) + (head // 2) % 2
    pages = jnp.swapaxes(cache[0], 1, 2).reshape(4, 2, width, cache.shape[2])

    def of_label(which):
        return lax.dynamic_index_in_dim(pages, which, 0, keepdims=False)

    def passed(which, ds, dz):
        pairs = [
            (
                s * n_head + h,
                (s + ds) % n_section * n_head + (h + 2 * dz) % n_head,
            )
            for s in range(n_section)
            for h in range(n_head)
        ]
        return lax.ppermute(of_label(which), SPLIT, pairs)

    moved = [passed(label ^ 2, 1, 0), passed(label ^ 1, 0, 1), passed(label ^ 3, -1, -1)]
    spread = queries[0].reshape(1, 2, 1, 2, 1, 2 * heads_dev, width)
    spread = jnp.broadcast_to(
        spread, (n_section // 2, 2, n_head // 4, 2, 2, 2 * heads_dev, width)
    )
    q_all = exchange(spread.reshape(n_shard * 2 * heads_dev, width), SPLIT)
    sent = run(
        functools.partial(attend_kernel, n_section, n_head),
        (q_all.shape[0], LAT + 128),
        kept_length,
        q_all,
        of_label(label),
        *moved,
        cost=32,
    )
    got = exchange(sent, SPLIT)
    term = run(
        functools.partial(project_kernel, n_section, n_head),
        (n_section, n_head, reqs, width_dev),
        got,
        w_uv,
        w_out,
        resid,
        cost=32,
    )
    terms = exchange(term.reshape(n_shard * reqs, width_dev), SPLIT)
    hidden = jnp.sum(terms.reshape(n_shard, reqs, width_dev).astype(f32), axis=0).astype(bf16)

    def from_group(d):
        return lax.ppermute(hidden, "group", [(g, g ^ d) for g in range(n_group)])

    others = [from_group(d) for d in range(1, n_group)]

    ff_dev = w_gate.shape[2] // n_head
    count = n_group * reqs
    both = run(
        expert_in_kernel, (n_head, count, 2 * ff_dev + 128), hidden, *others, w_gate, w_up
    )
    both = exchange(both, "head")
    act = run(act_kernel, (n_head, count, ff_dev), both)
    act = exchange(act, "head")
    served = run(
        functools.partial(expert_out_kernel, n_section, n_group),
        (n_expert, rows_dev, width_dev),
        act,
        w_down,
    )
    back = exchange(served, ("section", "group"))
    return run(finish_kernel, (1, rows_dev, width_dev), back, picks, pick_logits, hidden)


def solution(mesh):
    return jax.shard_map(
        local,
        mesh=mesh,
        in_specs=(
            P("group", None, ("section", "head"), None),
            P("group", None, ("section", "head"), None),
            P("group", None),
            P(("section", "head"), None, None),
            P(("section", "head"), None),
            P("group", "section", "head"),
            P("group", "section", None),
            P("group", "section", None),
            P(("section", "group"), "head", None),
            P(("section", "group"), "head", None),
            P(("section", "group"), None, "head"),
        ),
        out_specs=P("group", "section", "head"),
        check_vma=False,
    )
```

```python
import functools

import jax
import jax.numpy as jnp
from jax import lax
from jax.experimental import pallas as pl
from jax.experimental.pallas import tpu as pltpu
from jax.sharding import PartitionSpec as P

LAT = 512
ROPE = 64
VDIM = 128
D = 7168

neg_fill = -1e30
norm_eps = 1e-06
route_scale = 2.5
f32 = jnp.float32
bf16 = jnp.bfloat16
SPLIT = ("section", "head")
VMEM = pl.BlockSpec(memory_space=pltpu.VMEM)
FAR = pl.BlockSpec(memory_space=pltpu.HBM)
W_PARTS = 4


def exchange(x, axes):
    return lax.all_to_all(x, axes, split_axis=0, concat_axis=0, tiled=True)


def contract(a, b, dims):
    return lax.dot_general(a, b, (dims, ((), ())), preferred_element_type=f32)


def in_lanes(x):
    high = x.astype(bf16).astype(f32)
    rest = x - high
    middle = rest.astype(bf16).astype(f32)
    lane = lax.broadcasted_iota(jnp.int32, (x.shape[0], 128), 1)
    zero = jnp.zeros((x.shape[0], 128), f32)
    low = jnp.where(lane == 2, rest - middle, zero)
    return jnp.where(lane == 0, high, jnp.where(lane == 1, middle, low))


def copies(source, target, sems, parts):
    rows = target.shape[0] // parts
    return [
        pltpu.make_async_copy(
            source.at[pl.ds(i * rows, rows)], target.at[pl.ds(i * rows, rows)], sems.at[i]
        )
        for i in range(parts)
    ]


def start_all(moves):
    for move in moves:
        move.start()


def wait_all(moves):
    for move in moves:
        move.wait()


def label_here():
    return 2 * (lax.axis_index("section") % 2) + (lax.axis_index("head") // 2) % 2


def prepare_kernel(
    n_section, n_head, queries_ref, cache_ref, asked_ref, p1, p2, p3, q, q_sem, sems
):
    label = label_here()
    asked = pltpu.make_async_copy(queries_ref.at[0], q, q_sem)
    asked.start()
    moves = [
        pltpu.make_async_copy(cache_ref.at[label ^ d], p, sems.at[i])
        for i, (d, p) in enumerate(((2, p1), (1, p2), (3, p3)))
    ]
    start_all(moves)
    asked.wait()
    heads = q.shape[1]
    for which in range(4):
        rows = [q[2 * which + r].astype(f32) for r in range(2)]
        block = jnp.concatenate(rows, axis=0).astype(bf16)
        for s in range(which // 2, n_section, 2):
            for z in range(which % 2, n_head // 2, 2):
                for y in range(2):
                    asked_ref[s * n_head + 2 * z + y] = block
    wait_all(moves)


def attend_kernel(
    n_section,
    n_head,
    q_ref,
    k1,
    k2,
    k3,
    cache_ref,
    length_ref,
    out_w_ref,
    out_ref,
    early_ref,
    k0,
    length,
    sems,
    w_sems,
):
    section = lax.axis_index("section")
    head = lax.axis_index("head")
    label = label_here()
    own = pltpu.make_async_copy(cache_ref.at[label], k0, sems.at[0])
    own.start()
    lengths = pltpu.make_async_copy(length_ref, length, sems.at[1])
    lengths.start()
    weights_in = copies(out_w_ref, early_ref, w_sems, W_PARTS)
    start_all(weights_in)
    block = k0.shape[2]
    sources = (
        (section, head),
        ((section + n_section - 1) % n_section, head),
        (section, (head + n_head - 2) % n_head),
        ((section + 1) % n_section, (head + 2) % n_head),
    )
    rows = q_ref.shape[0]
    first = lax.broadcasted_iota(jnp.int32, (rows, 1), 0) % 8 < 4
    lane = lax.broadcasted_iota(jnp.int32, (1, block), 1)
    position = jnp.concatenate([(s * n_head + h) * block + lane for s, h in sources], axis=1)
    q = q_ref[...]
    own.wait()
    pages = [jnp.concatenate([k[r] for k in (k0, k1, k2, k3)], axis=1) for r in range(2)]
    scores = [contract(q, page, ((1,), (0,))) for page in pages]
    scores = jnp.where(first, scores[0], scores[1]) * ((VDIM + ROPE) ** -0.5)
    lengths.wait()
    limit = jnp.where(first, length[0, 2 * label], length[0, 2 * label + 1])
    counted = position < limit
    top = jnp.max(jnp.where(counted, scores, neg_fill), axis=1, keepdims=True)
    weights = jnp.where(counted, jnp.exp(scores - top), 0.0)
    total = jnp.sum(weights, axis=1, keepdims=True)
    weights = weights.astype(bf16)
    outs = [contract(weights, page[:LAT], ((1,), (1,))) for page in pages]
    any_kept = total > 0
    safe = jnp.where(any_kept, total, 1.0)
    out_ref[:, :LAT] = (jnp.where(first, outs[0], outs[1]) / safe).astype(bf16)
    level = jnp.where(any_kept, top + jnp.log(safe), neg_fill)
    out_ref[:, LAT:] = in_lanes(level).astype(bf16)
    wait_all(weights_in)


def project_kernel(
    n_section, n_head, got_ref, uv_ref, early_ref, out_w_ref, resid_ref, term_ref, late, w_sems
):
    reqs, width_dev = term_ref.shape[2:]
    half = late.shape[0]
    weights_in = copies(out_w_ref.at[pl.ds(half, half)], late, w_sems, W_PARTS)
    start_all(weights_in)
    got = got_ref[...].astype(f32).reshape(n_section * n_head, 8, LAT + 128)
    level = jnp.sum(got[:, :, LAT:], axis=2, keepdims=True)
    merged = []
    for label in range(4):
        parts = [
            (2 * a + label // 2) * n_head + 2 * (2 * b + label % 2) + c
            for a in range(n_section // 2)
            for b in range(n_head // 4)
            for c in range(2)
        ]
        top = functools.reduce(jnp.maximum, [level[d] for d in parts])
        share = [jnp.exp(level[d] - top) for d in parts]
        total = functools.reduce(jnp.add, share)
        mix = functools.reduce(jnp.add, [w * got[d, :, :LAT] for w, d in zip(share, parts)])
        merged.append(mix / total)
    latent = jnp.concatenate(merged, axis=0).astype(bf16)
    heads = uv_ref.shape[0]
    row = lax.broadcasted_iota(jnp.int32, (reqs, reqs * heads), 0)
    column = lax.broadcasted_iota(jnp.int32, (reqs, reqs * heads), 1)
    values = []
    for i in range(heads):
        pick = (column == heads * row + i).astype(f32).astype(bf16)
        own = contract(pick, latent, ((1,), (0,))).astype(bf16)
        values.append(contract(own, uv_ref[i], ((1,), (0,))))
    values = jnp.concatenate(values, axis=1).astype(bf16)
    row = lax.broadcasted_iota(jnp.int32, (reqs, width_dev), 0)
    resid = resid_ref[0].astype(f32)
    spread = jnp.where(row % 2 == 0, resid[0:1], resid[1:2])
    spread = jnp.where(row // 2 == lax.axis_index("section"), spread, 0.0)
    head = lax.axis_index("head")
    first = contract(values[:, :half], early_ref[...], ((1,), (0,)))
    wait_all(weights_in)
    for k in range(n_head):
        columns = slice(k * width_dev, (k + 1) * width_dev)
        term = first[:, columns] + contract(values[:, half:], late[:, columns], ((1,), (0,)))
        term = (term + jnp.where(head == k, spread, 0.0)).astype(bf16)
        for s in range(n_section):
            term_ref[s, k] = term


def fetch_kernel(after_ref, gate_ref, up_ref, gate_out, up_out, sems):
    moves = copies(gate_ref.at[0], gate_out, sems.at[0], W_PARTS)
    moves += copies(up_ref.at[0], up_out, sems.at[1], W_PARTS)
    start_all(moves)
    wait_all(moves)


def expert_in_kernel(r0, r1, r2, r3, gate_ref, up_ref, both_ref):
    wide = jnp.concatenate([r[...].astype(f32) for r in (r0, r1, r2, r3)], axis=0)
    rows = wide.astype(bf16)
    squares = in_lanes(jnp.sum(wide * wide, axis=1, keepdims=True)).astype(bf16)
    n_head = both_ref.shape[0]
    ff = gate_ref.shape[1] // n_head
    for k in range(n_head):
        columns = slice(k * ff, (k + 1) * ff)
        both_ref[k, :, :ff] = contract(rows, gate_ref[:, columns], ((1,), (0,))).astype(bf16)
        both_ref[k, :, ff : 2 * ff] = contract(
            rows, up_ref[:, columns], ((1,), (0,))
        ).astype(bf16)
        both_ref[k, :, 2 * ff :] = squares


def act_kernel(both_ref, act_ref):
    both = jnp.sum(both_ref[...].astype(f32), axis=0)
    ff = act_ref.shape[2]
    squares = jnp.sum(both[:, 2 * ff :], axis=1, keepdims=True)
    factor = lax.rsqrt(squares / D + norm_eps)
    gate = both[:, :ff] * factor
    act = gate * jax.nn.sigmoid(gate) * (both[:, ff : 2 * ff] * factor)
    act = act.astype(bf16)
    for k in range(act_ref.shape[0]):
        act_ref[k] = act


def expert_out_kernel(n_section, n_group, act_ref, down_ref, served_ref):
    n_head, _, ff = act_ref.shape
    act = jnp.concatenate([act_ref[k] for k in range(n_head)], axis=1)
    total = contract(act, down_ref[0], ((1,), (0,)))
    group = lax.axis_index("group")
    rows_dev = served_ref.shape[1]
    for d in range(n_group):
        for s in range(n_section):
            start = (d * n_section + s) * rows_dev
            served_ref[s * n_group + (group ^ d)] = total[start : start + rows_dev].astype(bf16)


def finish_kernel(back_ref, picks_ref, logits_ref, hidden_ref, out_ref):
    n_expert, rows_dev, width_dev = back_ref.shape
    affinity = jax.nn.sigmoid(logits_ref[0])
    share = route_scale * affinity / jnp.sum(affinity, axis=1, keepdims=True)
    expert = lax.broadcasted_iota(jnp.int32, (rows_dev, n_expert), 1)
    weight = jnp.zeros((rows_dev, n_expert), f32)
    picks = picks_ref[0]
    for k in range(picks.shape[1]):
        weight += jnp.where(picks[:, k : k + 1] == expert, share[:, k : k + 1], 0.0)
    hidden = hidden_ref[...].astype(f32)
    section = lax.axis_index("section")
    total = jnp.zeros((rows_dev, width_dev), f32)
    for s in range(hidden.shape[0] // rows_dev):
        total += jnp.where(section == s, hidden[s * rows_dev : (s + 1) * rows_dev], 0.0)
    mixture = jnp.zeros((rows_dev, width_dev), f32)
    for e in range(n_expert):
        mixture += weight[:, e : e + 1] * back_ref[e].astype(f32)
    out_ref[0] = (total + mixture).astype(bf16)


def run(kernel, shapes, *args, far=(), scratch=(), limit=16):
    single = isinstance(shapes[0], int)
    args = [
        pltpu.with_memory_space_constraint(a, pltpu.HBM) if i in far else a
        for i, a in enumerate(args)
    ]
    shapes = [jax.ShapeDtypeStruct(shape, bf16) for shape in ([shapes] if single else shapes)]
    return pl.pallas_call(
        kernel,
        out_shape=shapes[0] if single else shapes,
        in_specs=[FAR if i in far else VMEM for i in range(len(args))],
        out_specs=VMEM if single else [VMEM] * len(shapes),
        scratch_shapes=list(scratch),
        compiler_params=pltpu.CompilerParams(vmem_limit_bytes=limit * 1024 * 1024),
    )(*args)


def local(
    queries, cache, kept_length, w_uv, w_out, resid, picks, pick_logits, w_gate, w_up, w_down
):
    n_section = lax.axis_size("section")
    n_group = lax.axis_size("group")
    n_head = lax.axis_size("head")
    n_shard = n_section * n_head
    n_expert = n_section * n_group
    reqs, heads_dev, width = queries.shape[1:]
    rows_dev, width_dev = resid.shape[1:]

    block = cache.shape[2]
    pages = jnp.swapaxes(cache[0], 1, 2).reshape(4, 2, width, block)
    dma = pltpu.SemaphoreType.DMA

    def passed(part, ds, dz):
        pairs = [
            (
                s * n_head + h,
                (s + ds) % n_section * n_head + (h + 2 * dz) % n_head,
            )
            for s in range(n_section)
            for h in range(n_head)
        ]
        return lax.ppermute(part, SPLIT, pairs)

    asked, *parts = run(
        functools.partial(prepare_kernel, n_section, n_head),
        [(n_shard, 2 * heads_dev, width)] + [(2, width, block)] * 3,
        queries,
        pages,
        far=(0, 1),
        scratch=[pltpu.VMEM((reqs, heads_dev, width), bf16), dma(()), dma((3,))],
    )
    moved = [passed(part, *way) for part, way in zip(parts, ((1, 0), (0, 1), (-1, -1)))]
    q_all = exchange(asked.reshape(n_shard * 2 * heads_dev, width), SPLIT)
    half = (w_out.shape[0] // 2, w_out.shape[1])
    sent, early = run(
        functools.partial(attend_kernel, n_section, n_head),
        [(q_all.shape[0], LAT + 128), half],
        q_all,
        *moved,
        pages,
        kept_length,
        w_out,
        far=(4, 5, 6),
        scratch=[
            pltpu.VMEM((2, width, block), bf16),
            pltpu.SMEM(kept_length.shape, jnp.int32),
            dma((2,)),
            dma((W_PARTS,)),
        ],
    )
    got = exchange(sent, SPLIT)
    term = run(
        functools.partial(project_kernel, n_section, n_head),
        (n_section, n_head, reqs, width_dev),
        got,
        w_uv,
        early,
        w_out,
        resid,
        far=(3,),
        scratch=[pltpu.VMEM(half, bf16), dma((W_PARTS,))],
    )
    terms = exchange(term.reshape(n_shard * reqs, width_dev), SPLIT)
    hidden = jnp.sum(terms.reshape(n_shard, reqs, width_dev).astype(f32), axis=0).astype(bf16)

    def from_group(d):
        return lax.ppermute(hidden, "group", [(g, g ^ d) for g in range(n_group)])

    others = [from_group(d) for d in range(1, n_group)]

    ff_dev = w_gate.shape[2] // n_head
    count = n_group * reqs
    gate, up = run(
        fetch_kernel,
        [w_gate.shape[1:], w_up.shape[1:]],
        hidden,
        w_gate,
        w_up,
        far=(1, 2),
        scratch=[dma((2, W_PARTS))],
    )
    both = run(expert_in_kernel, (n_head, count, 2 * ff_dev + 128), hidden, *others, gate, up)
    both = exchange(both, "head")
    act = run(act_kernel, (n_head, count, ff_dev), both)
    act = exchange(act, "head")
    served = run(
        functools.partial(expert_out_kernel, n_section, n_group),
        (n_expert, rows_dev, width_dev),
        act,
        w_down,
    )
    back = exchange(served, ("section", "group"))
    return run(finish_kernel, (1, rows_dev, width_dev), back, picks, pick_logits, hidden)


def solution(mesh):
    return jax.shard_map(
        local,
        mesh=mesh,
        in_specs=(
            P("group", None, ("section", "head"), None),
            P("group", None, ("section", "head"), None),
            P("group", None),
            P(("section", "head"), None, None),
            P(("section", "head"), None),
            P("group", "section", "head"),
            P("group", "section", None),
            P("group", "section", None),
            P(("section", "group"), "head", None),
            P(("section", "group"), "head", None),
            P(("section", "group"), None, "head"),
        ),
        out_specs=P("group", "section", "head"),
        check_vma=False,
    )
```

```python
import functools

import jax
import jax.numpy as jnp
from jax import lax
from jax.experimental import pallas as pl
from jax.experimental.pallas import tpu as pltpu
from jax.sharding import PartitionSpec as P

LAT = 512
ROPE = 64
VDIM = 128
D = 7168

neg_fill = -1e30
norm_eps = 1e-06
route_scale = 2.5
f32 = jnp.float32
bf16 = jnp.bfloat16
SPLIT = ("section", "head")
VMEM = pl.BlockSpec(memory_space=pltpu.VMEM)
FAR = pl.BlockSpec(memory_space=pltpu.HBM)


def exchange(x, axes):
    return lax.all_to_all(x, axes, split_axis=0, concat_axis=0, tiled=True)


def contract(a, b, dims):
    return lax.dot_general(a, b, (dims, ((), ())), preferred_element_type=f32)


def in_lanes(x):
    high = x.astype(bf16).astype(f32)
    rest = x - high
    middle = rest.astype(bf16).astype(f32)
    lane = lax.broadcasted_iota(jnp.int32, (x.shape[0], 128), 1)
    zero = jnp.zeros((x.shape[0], 128), f32)
    low = jnp.where(lane == 2, rest - middle, zero)
    return jnp.where(lane == 0, high, jnp.where(lane == 1, middle, low))


def start_all(moves):
    for move in moves:
        move.start()


def wait_all(moves):
    for move in moves:
        move.wait()


def label_here():
    return 2 * (lax.axis_index("section") % 2) + (lax.axis_index("head") // 2) % 2


def prepare_kernel(
    n_section,
    n_head,
    queries_ref,
    cache_ref,
    length_ref,
    asked_ref,
    p0,
    p1,
    p2,
    p3,
    length,
    q,
    q_sem,
    sems,
):
    label = label_here()
    asked = pltpu.make_async_copy(queries_ref.at[0], q, q_sem)
    asked.start()
    moves = [
        pltpu.make_async_copy(cache_ref.at[label ^ d], p, sems.at[i])
        for i, (d, p) in enumerate(((2, p1), (1, p2), (3, p3), (0, p0)))
    ]
    moves.append(pltpu.make_async_copy(length_ref, length, sems.at[4]))
    start_all(moves)
    asked.wait()
    heads = q.shape[1]
    for which in range(4):
        rows = [q[2 * which + r].astype(f32) for r in range(2)]
        block = jnp.concatenate(rows, axis=0).astype(bf16)
        for s in range(which // 2, n_section, 2):
            for z in range(which % 2, n_head // 2, 2):
                for y in range(2):
                    asked_ref[s * n_head + 2 * z + y] = block
    wait_all(moves)


def attend_kernel(
    n_section,
    n_head,
    q_ref,
    length_ref,
    k0,
    k1,
    k2,
    k3,
    ahead_ref,
    out_ref,
):
    section = lax.axis_index("section")
    head = lax.axis_index("head")
    label = label_here()
    block = k0.shape[2]
    sources = (
        (section, head),
        ((section + n_section - 1) % n_section, head),
        (section, (head + n_head - 2) % n_head),
        ((section + 1) % n_section, (head + 2) % n_head),
    )
    rows = q_ref.shape[0]
    first = lax.broadcasted_iota(jnp.int32, (rows, 1), 0) % 8 < 4
    lane = lax.broadcasted_iota(jnp.int32, (1, block), 1)
    position = jnp.concatenate([(s * n_head + h) * block + lane for s, h in sources], axis=1)
    q = q_ref[...]
    pages = [jnp.concatenate([k[r] for k in (k0, k1, k2, k3)], axis=1) for r in range(2)]
    scores = [contract(q, page, ((1,), (0,))) for page in pages]
    scores = jnp.where(first, scores[0], scores[1]) * ((VDIM + ROPE) ** -0.5)
    length = length_ref[...]
    named = lax.broadcasted_iota(jnp.int32, length.shape, 1) - 2 * label
    limit = [jnp.sum(jnp.where(named == r, length, 0), axis=1, keepdims=True) for r in range(2)]
    limit = jnp.where(first, limit[0], limit[1])
    counted = position < limit
    top = jnp.max(jnp.where(counted, scores, neg_fill), axis=1, keepdims=True)
    weights = jnp.where(counted, jnp.exp(scores - top), 0.0)
    total = jnp.sum(weights, axis=1, keepdims=True)
    weights = weights.astype(bf16)
    outs = [contract(weights, page[:LAT], ((1,), (1,))) for page in pages]
    any_kept = total > 0
    safe = jnp.where(any_kept, total, 1.0)
    out_ref[:, :LAT] = (jnp.where(first, outs[0], outs[1]) / safe).astype(bf16)
    level = jnp.where(any_kept, top + jnp.log(safe), neg_fill)
    out_ref[:, LAT:] = in_lanes(level).astype(bf16)


def project_kernel(
    n_section, n_head, got_ref, uv_ref, out_w_ref, resid_ref, ahead_gate, ahead_up, term_ref
):
    reqs, width_dev = term_ref.shape[2:]
    got = got_ref[...].astype(f32).reshape(n_section * n_head, 8, LAT + 128)
    level = jnp.sum(got[:, :, LAT:], axis=2, keepdims=True)
    merged = []
    for label in range(4):
        parts = [
            (2 * a + label // 2) * n_head + 2 * (2 * b + label % 2) + c
            for a in range(n_section // 2)
            for b in range(n_head // 4)
            for c in range(2)
        ]
        top = functools.reduce(jnp.maximum, [level[d] for d in parts])
        share = [jnp.exp(level[d] - top) for d in parts]
        total = functools.reduce(jnp.add, share)
        mix = functools.reduce(jnp.add, [w * got[d, :, :LAT] for w, d in zip(share, parts)])
        merged.append(mix / total)
    latent = jnp.concatenate(merged, axis=0).astype(bf16)
    heads = uv_ref.shape[0]
    row = lax.broadcasted_iota(jnp.int32, (reqs, reqs * heads), 0)
    column = lax.broadcasted_iota(jnp.int32, (reqs, reqs * heads), 1)
    values = []
    for i in range(heads):
        pick = (column == heads * row + i).astype(f32).astype(bf16)
        own = contract(pick, latent, ((1,), (0,))).astype(bf16)
        values.append(contract(own, uv_ref[i], ((1,), (0,))))
    values = jnp.concatenate(values, axis=1).astype(bf16)
    row = lax.broadcasted_iota(jnp.int32, (reqs, width_dev), 0)
    resid = resid_ref[0].astype(f32)
    spread = jnp.where(row % 2 == 0, resid[0:1], resid[1:2])
    spread = jnp.where(row // 2 == lax.axis_index("section"), spread, 0.0)
    head = lax.axis_index("head")
    for k in range(n_head):
        columns = slice(k * width_dev, (k + 1) * width_dev)
        term = contract(values, out_w_ref[:, columns], ((1,), (0,)))
        term = (term + jnp.where(head == k, spread, 0.0)).astype(bf16)
        for s in range(n_section):
            term_ref[s, k] = term


def rows_kernel(terms_ref, hidden_ref):
    reqs, width_dev = hidden_ref.shape
    terms = terms_ref[...].astype(f32).reshape(-1, reqs, width_dev)
    hidden_ref[...] = jnp.sum(terms, axis=0).astype(bf16)


def weigh_kernel(hidden_ref, picks_ref, logits_ref, weight_ref, mine_ref):
    rows_dev, n_expert = weight_ref.shape
    affinity = jax.nn.sigmoid(logits_ref[0])
    share = route_scale * affinity / jnp.sum(affinity, axis=1, keepdims=True)
    expert = lax.broadcasted_iota(jnp.int32, (rows_dev, n_expert), 1)
    weight = jnp.zeros((rows_dev, n_expert), f32)
    picks = picks_ref[0]
    for k in range(picks.shape[1]):
        weight += jnp.where(picks[:, k : k + 1] == expert, share[:, k : k + 1], 0.0)
    weight_ref[...] = weight
    hidden = hidden_ref[...].astype(f32)
    section = lax.axis_index("section")
    total = jnp.zeros(mine_ref.shape, f32)
    for s in range(hidden.shape[0] // rows_dev):
        total += jnp.where(section == s, hidden[s * rows_dev : (s + 1) * rows_dev], 0.0)
    mine_ref[...] = total


def expert_in_kernel(r0, r1, r2, r3, gate_ref, up_ref, after_ref, both_ref):
    wide = jnp.concatenate([r[...].astype(f32) for r in (r0, r1, r2, r3)], axis=0)
    rows = wide.astype(bf16)
    squares = in_lanes(jnp.sum(wide * wide, axis=1, keepdims=True)).astype(bf16)
    n_head = both_ref.shape[0]
    ff = gate_ref.shape[2] // n_head
    for k in range(n_head):
        columns = slice(k * ff, (k + 1) * ff)
        both_ref[k, :, :ff] = contract(rows, gate_ref[0, :, columns], ((1,), (0,))).astype(bf16)
        both_ref[k, :, ff : 2 * ff] = contract(
            rows, up_ref[0, :, columns], ((1,), (0,))
        ).astype(bf16)
        both_ref[k, :, 2 * ff :] = squares


def act_kernel(both_ref, act_ref):
    both = jnp.sum(both_ref[...].astype(f32), axis=0)
    ff = act_ref.shape[2]
    squares = jnp.sum(both[:, 2 * ff :], axis=1, keepdims=True)
    factor = lax.rsqrt(squares / D + norm_eps)
    gate = both[:, :ff] * factor
    act = gate * jax.nn.sigmoid(gate) * (both[:, ff : 2 * ff] * factor)
    act = act.astype(bf16)
    for k in range(act_ref.shape[0]):
        act_ref[k] = act


def expert_out_kernel(n_section, n_group, act_ref, down_ref, served_ref):
    n_head, _, ff = act_ref.shape
    act = jnp.concatenate([act_ref[k] for k in range(n_head)], axis=1)
    total = contract(act, down_ref[0], ((1,), (0,)))
    group = lax.axis_index("group")
    rows_dev = served_ref.shape[1]
    for d in range(n_group):
        for s in range(n_section):
            start = (d * n_section + s) * rows_dev
            served_ref[s * n_group + (group ^ d)] = total[start : start + rows_dev].astype(bf16)


def finish_kernel(back_ref, weight_ref, mine_ref, out_ref):
    weight = weight_ref[...]
    total = mine_ref[...]
    for e in range(back_ref.shape[0]):
        total += weight[:, e : e + 1] * back_ref[e].astype(f32)
    out_ref[0] = total.astype(bf16)


def run(kernel, shapes, *args, far=(), scratch=(), limit=16):
    single = isinstance(shapes[0], int)
    args = [
        pltpu.with_memory_space_constraint(a, pltpu.HBM) if i in far else a
        for i, a in enumerate(args)
    ]
    shapes = [
        jax.ShapeDtypeStruct(shape, bf16) if isinstance(shape, tuple) else shape
        for shape in ([shapes] if single else shapes)
    ]
    return pl.pallas_call(
        kernel,
        out_shape=shapes[0] if single else shapes,
        in_specs=[FAR if i in far else VMEM for i in range(len(args))],
        out_specs=VMEM if single else [VMEM] * len(shapes),
        scratch_shapes=list(scratch),
        compiler_params=pltpu.CompilerParams(vmem_limit_bytes=limit * 1024 * 1024),
    )(*args)


def local(
    queries, cache, kept_length, w_uv, w_out, resid, picks, pick_logits, w_gate, w_up, w_down
):
    n_section = lax.axis_size("section")
    n_group = lax.axis_size("group")
    n_head = lax.axis_size("head")
    n_shard = n_section * n_head
    n_expert = n_section * n_group
    reqs, heads_dev, width = queries.shape[1:]
    rows_dev, width_dev = resid.shape[1:]

    block = cache.shape[2]
    pages = jnp.swapaxes(cache[0], 1, 2).reshape(4, 2, width, block)
    dma = pltpu.SemaphoreType.DMA

    def passed(part, ds, dz):
        pairs = [
            (
                s * n_head + h,
                (s + ds) % n_section * n_head + (h + 2 * dz) % n_head,
            )
            for s in range(n_section)
            for h in range(n_head)
        ]
        return lax.ppermute(part, SPLIT, pairs)

    asked, own, *parts, lengths = run(
        functools.partial(prepare_kernel, n_section, n_head),
        [(n_shard, 2 * heads_dev, width)]
        + [(2, width, block)] * 4
        + [jax.ShapeDtypeStruct(kept_length.shape, jnp.int32)],
        queries,
        pages,
        kept_length,
        far=(0, 1, 2),
        scratch=[pltpu.VMEM((reqs, heads_dev, width), bf16), dma(()), dma((5,))],
    )
    moved = [passed(part, *way) for part, way in zip(parts, ((1, 0), (0, 1), (-1, -1)))]
    q_all = exchange(asked.reshape(n_shard * 2 * heads_dev, width), SPLIT)
    sent = run(
        functools.partial(attend_kernel, n_section, n_head),
        (q_all.shape[0], LAT + 128),
        q_all,
        lengths,
        own,
        *moved,
        w_out,
        far=(6,),
    )
    got = exchange(sent, SPLIT)
    term = run(
        functools.partial(project_kernel, n_section, n_head),
        (n_section, n_head, reqs, width_dev),
        got,
        w_uv,
        w_out,
        resid,
        w_gate,
        w_up,
        far=(4, 5),
    )
    terms = exchange(term.reshape(n_shard * reqs, width_dev), SPLIT)
    hidden = run(rows_kernel, (reqs, width_dev), terms)

    def from_group(d):
        return lax.ppermute(hidden, "group", [(g, g ^ d) for g in range(n_group)])

    others = [from_group(d) for d in range(1, n_group)]

    weight, mine = run(
        weigh_kernel,
        [
            jax.ShapeDtypeStruct((rows_dev, n_expert), f32),
            jax.ShapeDtypeStruct((rows_dev, width_dev), f32),
        ],
        hidden,
        picks,
        pick_logits,
    )

    ff_dev = w_gate.shape[2] // n_head
    count = n_group * reqs
    both = run(
        expert_in_kernel,
        (n_head, count, 2 * ff_dev + 128),
        hidden,
        *others,
        w_gate,
        w_up,
        mine,
    )
    both = exchange(both, "head")
    act = run(act_kernel, (n_head, count, ff_dev), both)
    act = exchange(act, "head")
    served = run(
        functools.partial(expert_out_kernel, n_section, n_group),
        (n_expert, rows_dev, width_dev),
        act,
        w_down,
    )
    back = exchange(served, ("section", "group"))
    return run(finish_kernel, (1, rows_dev, width_dev), back, weight, mine)


def solution(mesh):
    return jax.shard_map(
        local,
        mesh=mesh,
        in_specs=(
            P("group", None, ("section", "head"), None),
            P("group", None, ("section", "head"), None),
            P("group", None),
            P(("section", "head"), None, None),
            P(("section", "head"), None),
            P("group", "section", "head"),
            P("group", "section", None),
            P("group", "section", None),
            P(("section", "group"), "head", None),
            P(("section", "group"), "head", None),
            P(("section", "group"), None, "head"),
        ),
        out_specs=P("group", "section", "head"),
        check_vma=False,
    )
```

```python
import functools

import jax
import jax.numpy as jnp
from jax import lax
from jax.experimental import pallas as pl
from jax.experimental.pallas import tpu as pltpu
from jax.sharding import PartitionSpec as P

LAT = 512
ROPE = 64
VDIM = 128
D = 7168

neg_fill = -1e30
norm_eps = 1e-06
route_scale = 2.5
f32 = jnp.float32
bf16 = jnp.bfloat16
SPLIT = ("section", "head")
VMEM = pl.BlockSpec(memory_space=pltpu.VMEM)
FAR = pl.BlockSpec(memory_space=pltpu.HBM)


def exchange(x, axes):
    return lax.all_to_all(x, axes, split_axis=0, concat_axis=0, tiled=True)


def contract(a, b, dims):
    return lax.dot_general(a, b, (dims, ((), ())), preferred_element_type=f32)


def in_lanes(x):
    high = x.astype(bf16).astype(f32)
    rest = x - high
    middle = rest.astype(bf16).astype(f32)
    lane = lax.broadcasted_iota(jnp.int32, (x.shape[0], 128), 1)
    zero = jnp.zeros((x.shape[0], 128), f32)
    low = jnp.where(lane == 2, rest - middle, zero)
    return jnp.where(lane == 0, high, jnp.where(lane == 1, middle, low))


def start_all(moves):
    for move in moves:
        move.start()


def wait_all(moves):
    for move in moves:
        move.wait()


def label_here():
    return 2 * (lax.axis_index("section") % 2) + (lax.axis_index("head") // 2) % 2


def prepare_kernel(
    n_section,
    n_head,
    queries_ref,
    cache_ref,
    length_ref,
    asked_ref,
    p0,
    p1,
    p2,
    p3,
    length,
    q,
    q_sem,
    sems,
):
    label = label_here()
    asked = pltpu.make_async_copy(queries_ref.at[0], q, q_sem)
    asked.start()
    moves = [
        pltpu.make_async_copy(cache_ref.at[label ^ d], p, sems.at[i])
        for i, (d, p) in enumerate(((2, p1), (1, p2), (3, p3), (0, p0)))
    ]
    moves.append(pltpu.make_async_copy(length_ref, length, sems.at[4]))
    start_all(moves)
    asked.wait()
    heads = q.shape[1]
    for which in range(4):
        rows = [q[2 * which + r].astype(f32) for r in range(2)]
        block = jnp.concatenate(rows, axis=0).astype(bf16)
        for s in range(which // 2, n_section, 2):
            for z in range(which % 2, n_head // 2, 2):
                for y in range(2):
                    asked_ref[s * n_head + 2 * z + y] = block
    wait_all(moves)


def attend_kernel(
    n_section,
    n_head,
    q_ref,
    length_ref,
    k0,
    k1,
    k2,
    k3,
    ahead_ref,
    out_ref,
):
    section = lax.axis_index("section")
    head = lax.axis_index("head")
    label = label_here()
    block = k0.shape[2]
    sources = (
        (section, head),
        ((section + n_section - 1) % n_section, head),
        (section, (head + n_head - 2) % n_head),
        ((section + 1) % n_section, (head + 2) % n_head),
    )
    rows = q_ref.shape[0]
    first = lax.broadcasted_iota(jnp.int32, (rows, 1), 0) % 8 < 4
    lane = lax.broadcasted_iota(jnp.int32, (1, block), 1)
    position = jnp.concatenate([(s * n_head + h) * block + lane for s, h in sources], axis=1)
    q = q_ref[...]
    pages = [jnp.concatenate([k[r] for k in (k0, k1, k2, k3)], axis=1) for r in range(2)]
    scores = [contract(q, page, ((1,), (0,))) for page in pages]
    scores = jnp.where(first, scores[0], scores[1]) * ((VDIM + ROPE) ** -0.5)
    length = length_ref[...]
    named = lax.broadcasted_iota(jnp.int32, length.shape, 1) - 2 * label
    limit = [jnp.sum(jnp.where(named == r, length, 0), axis=1, keepdims=True) for r in range(2)]
    limit = jnp.where(first, limit[0], limit[1])
    counted = position < limit
    top = jnp.max(jnp.where(counted, scores, neg_fill), axis=1, keepdims=True)
    weights = jnp.where(counted, jnp.exp(scores - top), 0.0)
    total = jnp.sum(weights, axis=1, keepdims=True)
    weights = weights.astype(bf16)
    outs = [contract(weights, page[:LAT], ((1,), (1,))) for page in pages]
    any_kept = total > 0
    safe = jnp.where(any_kept, total, 1.0)
    out_ref[:, :LAT] = (jnp.where(first, outs[0], outs[1]) / safe).astype(bf16)
    level = jnp.where(any_kept, top + jnp.log(safe), neg_fill)
    out_ref[:, LAT:] = in_lanes(level).astype(bf16)


def project_kernel(
    n_section, n_head, got_ref, uv_ref, out_w_ref, resid_ref, ahead_gate, ahead_up, term_ref
):
    reqs, width_dev = term_ref.shape[2:]
    got = got_ref[...].astype(f32).reshape(n_section * n_head, 8, LAT + 128)
    level = jnp.sum(got[:, :, LAT:], axis=2, keepdims=True)
    merged = []
    for label in range(4):
        parts = [
            (2 * a + label // 2) * n_head + 2 * (2 * b + label % 2) + c
            for a in range(n_section // 2)
            for b in range(n_head // 4)
            for c in range(2)
        ]
        top = functools.reduce(jnp.maximum, [level[d] for d in parts])
        share = [jnp.exp(level[d] - top) for d in parts]
        total = functools.reduce(jnp.add, share)
        mix = functools.reduce(jnp.add, [w * got[d, :, :LAT] for w, d in zip(share, parts)])
        merged.append(mix / total)
    latent = jnp.concatenate(merged, axis=0).astype(bf16)
    heads = uv_ref.shape[0]
    row = lax.broadcasted_iota(jnp.int32, (reqs, reqs * heads), 0)
    column = lax.broadcasted_iota(jnp.int32, (reqs, reqs * heads), 1)
    values = []
    for i in range(heads):
        pick = (column == heads * row + i).astype(f32).astype(bf16)
        own = contract(pick, latent, ((1,), (0,))).astype(bf16)
        values.append(contract(own, uv_ref[i], ((1,), (0,))))
    values = jnp.concatenate(values, axis=1).astype(bf16)
    row = lax.broadcasted_iota(jnp.int32, (reqs, width_dev), 0)
    resid = resid_ref[0].astype(f32)
    spread = jnp.where(row % 2 == 0, resid[0:1], resid[1:2])
    spread = jnp.where(row // 2 == lax.axis_index("section"), spread, 0.0)
    head = lax.axis_index("head")
    for k in range(n_head):
        columns = slice(k * width_dev, (k + 1) * width_dev)
        term = contract(values, out_w_ref[:, columns], ((1,), (0,)))
        term = (term + jnp.where(head == k, spread, 0.0)).astype(bf16)
        for s in range(n_section):
            term_ref[s, k] = term


def rows_kernel(terms_ref, hidden_ref):
    reqs, width_dev = hidden_ref.shape
    terms = terms_ref[...].astype(f32).reshape(-1, reqs, width_dev)
    hidden_ref[...] = jnp.sum(terms, axis=0).astype(bf16)


def weigh_kernel(hidden_ref, picks_ref, logits_ref, weight_ref, mine_ref):
    rows_dev, n_expert = weight_ref.shape
    affinity = jax.nn.sigmoid(logits_ref[0])
    share = route_scale * affinity / jnp.sum(affinity, axis=1, keepdims=True)
    expert = lax.broadcasted_iota(jnp.int32, (rows_dev, n_expert), 1)
    weight = jnp.zeros((rows_dev, n_expert), f32)
    picks = picks_ref[0]
    for k in range(picks.shape[1]):
        weight += jnp.where(picks[:, k : k + 1] == expert, share[:, k : k + 1], 0.0)
    weight_ref[...] = weight
    hidden = hidden_ref[...].astype(f32)
    section = lax.axis_index("section")
    total = jnp.zeros(mine_ref.shape, f32)
    for s in range(hidden.shape[0] // rows_dev):
        total += jnp.where(section == s, hidden[s * rows_dev : (s + 1) * rows_dev], 0.0)
    mine_ref[...] = total


def expert_in_kernel(r0, r1, r2, r3, gate_ref, up_ref, after_ref, both_ref):
    wide = jnp.concatenate([r[...].astype(f32) for r in (r0, r1, r2, r3)], axis=0)
    rows = wide.astype(bf16)
    squares = jnp.sum(wide * wide, axis=1, keepdims=True)
    squares = jnp.sum(jnp.where(diagonal(rows.shape[0]), squares, 0.0), axis=0, keepdims=True)
    high = squares.astype(bf16).astype(f32)
    middle = (squares - high).astype(bf16).astype(f32)
    row = lax.broadcasted_iota(jnp.int32, (8, 128), 0)
    low = jnp.where(row == 2, squares - high - middle, 0.0)
    squares = jnp.where(row == 0, high, jnp.where(row == 1, middle, low))
    n_head = both_ref.shape[0]
    ff = gate_ref.shape[2] // n_head
    for k in range(n_head):
        columns = slice(k * ff, (k + 1) * ff)
        parts = []
        for w in (gate_ref, up_ref):
            sums = contract(rows, w[0, :, columns], ((1,), (0,)))
            parts += [sums[:, c : c + 128] for c in range(0, ff, 128)]
        both_ref[k] = jnp.concatenate(parts + [squares], axis=0).astype(bf16)


def diagonal(rows):
    row = lax.broadcasted_iota(jnp.int32, (rows, 128), 0)
    return row == lax.broadcasted_iota(jnp.int32, (rows, 128), 1)


def act_kernel(both_ref, act_ref):
    both = jnp.sum(both_ref[...].astype(f32), axis=0)
    count, ff = act_ref.shape[1:]
    blocks = [both[i * count : (i + 1) * count] for i in range(2 * ff // 128)]
    squares = jnp.sum(both[2 * ff // 128 * count :], axis=0, keepdims=True)
    squares = jnp.sum(jnp.where(diagonal(count), squares, 0.0), axis=1, keepdims=True)
    factor = lax.rsqrt(squares / D + norm_eps)
    gate = jnp.concatenate(blocks[: ff // 128], axis=1) * factor
    up = jnp.concatenate(blocks[ff // 128 :], axis=1) * factor
    act = (gate * jax.nn.sigmoid(gate) * up).astype(bf16)
    for k in range(act_ref.shape[0]):
        act_ref[k] = act


def expert_out_kernel(n_section, n_group, act_ref, down_ref, served_ref):
    n_head, _, ff = act_ref.shape
    act = jnp.concatenate([act_ref[k] for k in range(n_head)], axis=1)
    total = contract(act, down_ref[0], ((1,), (0,)))
    group = lax.axis_index("group")
    rows_dev = served_ref.shape[1]
    for d in range(n_group):
        for s in range(n_section):
            start = (d * n_section + s) * rows_dev
            served_ref[s * n_group + (group ^ d)] = total[start : start + rows_dev].astype(bf16)


def finish_kernel(back_ref, weight_ref, mine_ref, out_ref):
    weight = weight_ref[...]
    total = mine_ref[...]
    for e in range(back_ref.shape[0]):
        total += weight[:, e : e + 1] * back_ref[e].astype(f32)
    out_ref[0] = total.astype(bf16)


def run(kernel, shapes, *args, far=(), scratch=(), limit=16):
    single = isinstance(shapes[0], int)
    args = [
        pltpu.with_memory_space_constraint(a, pltpu.HBM) if i in far else a
        for i, a in enumerate(args)
    ]
    shapes = [
        jax.ShapeDtypeStruct(shape, bf16) if isinstance(shape, tuple) else shape
        for shape in ([shapes] if single else shapes)
    ]
    return pl.pallas_call(
        kernel,
        out_shape=shapes[0] if single else shapes,
        in_specs=[FAR if i in far else VMEM for i in range(len(args))],
        out_specs=VMEM if single else [VMEM] * len(shapes),
        scratch_shapes=list(scratch),
        compiler_params=pltpu.CompilerParams(vmem_limit_bytes=limit * 1024 * 1024),
    )(*args)


def local(
    queries, cache, kept_length, w_uv, w_out, resid, picks, pick_logits, w_gate, w_up, w_down
):
    n_section = lax.axis_size("section")
    n_group = lax.axis_size("group")
    n_head = lax.axis_size("head")
    n_shard = n_section * n_head
    n_expert = n_section * n_group
    reqs, heads_dev, width = queries.shape[1:]
    rows_dev, width_dev = resid.shape[1:]

    block = cache.shape[2]
    pages = jnp.swapaxes(cache[0], 1, 2).reshape(4, 2, width, block)
    dma = pltpu.SemaphoreType.DMA

    def passed(part, ds, dz):
        pairs = [
            (
                s * n_head + h,
                (s + ds) % n_section * n_head + (h + 2 * dz) % n_head,
            )
            for s in range(n_section)
            for h in range(n_head)
        ]
        return lax.ppermute(part, SPLIT, pairs)

    asked, own, *parts, lengths = run(
        functools.partial(prepare_kernel, n_section, n_head),
        [(n_shard, 2 * heads_dev, width)]
        + [(2, width, block)] * 4
        + [jax.ShapeDtypeStruct(kept_length.shape, jnp.int32)],
        queries,
        pages,
        kept_length,
        far=(0, 1, 2),
        scratch=[pltpu.VMEM((reqs, heads_dev, width), bf16), dma(()), dma((5,))],
    )
    moved = [passed(part, *way) for part, way in zip(parts, ((1, 0), (0, 1), (-1, -1)))]
    q_all = exchange(asked.reshape(n_shard * 2 * heads_dev, width), SPLIT)
    sent = run(
        functools.partial(attend_kernel, n_section, n_head),
        (q_all.shape[0], LAT + 128),
        q_all,
        lengths,
        own,
        *moved,
        w_out,
        far=(6,),
    )
    got = exchange(sent, SPLIT)
    term = run(
        functools.partial(project_kernel, n_section, n_head),
        (n_section, n_head, reqs, width_dev),
        got,
        w_uv,
        w_out,
        resid,
        w_gate,
        w_up,
        far=(4, 5),
    )
    terms = exchange(term.reshape(n_shard * reqs, width_dev), SPLIT)
    hidden = run(rows_kernel, (reqs, width_dev), terms)

    def from_group(d):
        return lax.ppermute(hidden, "group", [(g, g ^ d) for g in range(n_group)])

    others = [from_group(d) for d in range(1, n_group)]

    weight, mine = run(
        weigh_kernel,
        [
            jax.ShapeDtypeStruct((rows_dev, n_expert), f32),
            jax.ShapeDtypeStruct((rows_dev, width_dev), f32),
        ],
        hidden,
        picks,
        pick_logits,
    )

    ff_dev = w_gate.shape[2] // n_head
    count = n_group * reqs
    both = run(
        expert_in_kernel,
        (n_head, 2 * ff_dev // 128 * count + 8, 128),
        hidden,
        *others,
        w_gate,
        w_up,
        mine,
    )
    both = exchange(both, "head")
    act = run(act_kernel, (n_head, count, ff_dev), both)
    act = exchange(act, "head")
    served = run(
        functools.partial(expert_out_kernel, n_section, n_group),
        (n_expert, rows_dev, width_dev),
        act,
        w_down,
    )
    back = exchange(served, ("section", "group"))
    return run(finish_kernel, (1, rows_dev, width_dev), back, weight, mine)


def solution(mesh):
    return jax.shard_map(
        local,
        mesh=mesh,
        in_specs=(
            P("group", None, ("section", "head"), None),
            P("group", None, ("section", "head"), None),
            P("group", None),
            P(("section", "head"), None, None),
            P(("section", "head"), None),
            P("group", "section", "head"),
            P("group", "section", None),
            P("group", "section", None),
            P(("section", "group"), "head", None),
            P(("section", "group"), "head", None),
            P(("section", "group"), None, "head"),
        ),
        out_specs=P("group", "section", "head"),
        check_vma=False,
    )
```

```python
import functools

import jax
import jax.numpy as jnp
from jax import lax
from jax.experimental import pallas as pl
from jax.experimental.pallas import tpu as pltpu
from jax.sharding import PartitionSpec as P

LAT = 512
ROPE = 64
VDIM = 128
D = 7168

neg_fill = -1e30
norm_eps = 1e-06
route_scale = 2.5
f32 = jnp.float32
bf16 = jnp.bfloat16
SPLIT = ("section", "head")
VMEM = pl.BlockSpec(memory_space=pltpu.VMEM)
FAR = pl.BlockSpec(memory_space=pltpu.HBM)


def exchange(x, axes):
    return lax.all_to_all(x, axes, split_axis=0, concat_axis=0, tiled=True)


def contract(a, b, dims):
    return lax.dot_general(a, b, (dims, ((), ())), preferred_element_type=f32)


def in_lanes(x):
    high = x.astype(bf16).astype(f32)
    rest = x - high
    middle = rest.astype(bf16).astype(f32)
    lane = lax.broadcasted_iota(jnp.int32, (x.shape[0], 128), 1)
    zero = jnp.zeros((x.shape[0], 128), f32)
    low = jnp.where(lane == 2, rest - middle, zero)
    return jnp.where(lane == 0, high, jnp.where(lane == 1, middle, low))


def start_all(moves):
    for move in moves:
        move.start()


def wait_all(moves):
    for move in moves:
        move.wait()


def label_here():
    return 2 * (lax.axis_index("section") % 2) + (lax.axis_index("head") // 2) % 2


def prepare_kernel(
    n_section,
    n_head,
    queries_ref,
    cache_ref,
    length_ref,
    asked_ref,
    p0,
    p1,
    p2,
    p3,
    length,
    q,
    q_sem,
    sems,
):
    label = label_here()
    asked = pltpu.make_async_copy(queries_ref.at[0], q, q_sem)
    asked.start()
    moves = [
        pltpu.make_async_copy(cache_ref.at[label ^ d], p, sems.at[i])
        for i, (d, p) in enumerate(((2, p1), (1, p2), (3, p3), (0, p0)))
    ]
    moves.append(pltpu.make_async_copy(length_ref, length, sems.at[4]))
    start_all(moves)
    asked.wait()
    heads = q.shape[1]
    for which in range(4):
        rows = [q[2 * which + r].astype(f32) for r in range(2)]
        block = jnp.concatenate(rows, axis=0).astype(bf16)
        for s in range(which // 2, n_section, 2):
            for z in range(which % 2, n_head // 2, 2):
                for y in range(2):
                    asked_ref[s * n_head + 2 * z + y] = block
    wait_all(moves)


def attend_kernel(
    n_section,
    n_head,
    q_ref,
    length_ref,
    k0,
    k1,
    k2,
    k3,
    ahead_ref,
    out_ref,
):
    section = lax.axis_index("section")
    head = lax.axis_index("head")
    label = label_here()
    block = k0.shape[2]
    sources = (
        (section, head),
        ((section + n_section - 1) % n_section, head),
        (section, (head + n_head - 2) % n_head),
        ((section + 1) % n_section, (head + 2) % n_head),
    )
    rows = q_ref.shape[0]
    first = lax.broadcasted_iota(jnp.int32, (rows, 1), 0) % 8 < 4
    lane = lax.broadcasted_iota(jnp.int32, (1, block), 1)
    position = jnp.concatenate([(s * n_head + h) * block + lane for s, h in sources], axis=1)
    q = q_ref[...]
    pages = [jnp.concatenate([k[r] for k in (k0, k1, k2, k3)], axis=1) for r in range(2)]
    scores = [contract(q, page, ((1,), (0,))) for page in pages]
    scores = jnp.where(first, scores[0], scores[1]) * ((VDIM + ROPE) ** -0.5)
    length = length_ref[...]
    named = lax.broadcasted_iota(jnp.int32, length.shape, 1) - 2 * label
    limit = [jnp.sum(jnp.where(named == r, length, 0), axis=1, keepdims=True) for r in range(2)]
    limit = jnp.where(first, limit[0], limit[1])
    counted = position < limit
    top = jnp.max(jnp.where(counted, scores, neg_fill), axis=1, keepdims=True)
    weights = jnp.where(counted, jnp.exp(scores - top), 0.0)
    total = jnp.sum(weights, axis=1, keepdims=True)
    weights = weights.astype(bf16)
    outs = [contract(weights, page[:LAT], ((1,), (1,))) for page in pages]
    any_kept = total > 0
    safe = jnp.where(any_kept, total, 1.0)
    out_ref[:, :LAT] = (jnp.where(first, outs[0], outs[1]) / safe).astype(bf16)
    level = jnp.where(any_kept, top + jnp.log(safe), neg_fill)
    out_ref[:, LAT:] = in_lanes(level).astype(bf16)


def project_kernel(
    n_section, n_head, got_ref, uv_ref, out_w_ref, resid_ref, ahead_gate, ahead_up, term_ref
):
    reqs, width_dev = term_ref.shape[2:]
    got = got_ref[...].astype(f32).reshape(n_section * n_head, 8, LAT + 128)
    level = jnp.sum(got[:, :, LAT:], axis=2, keepdims=True)
    merged = []
    for label in range(4):
        parts = [
            (2 * a + label // 2) * n_head + 2 * (2 * b + label % 2) + c
            for a in range(n_section // 2)
            for b in range(n_head // 4)
            for c in range(2)
        ]
        top = functools.reduce(jnp.maximum, [level[d] for d in parts])
        share = [jnp.exp(level[d] - top) for d in parts]
        total = functools.reduce(jnp.add, share)
        mix = functools.reduce(jnp.add, [w * got[d, :, :LAT] for w, d in zip(share, parts)])
        merged.append(mix / total)
    latent = jnp.concatenate(merged, axis=0).astype(bf16)
    heads = uv_ref.shape[0]
    maps = jnp.concatenate([uv_ref[i] for i in range(heads)], axis=1)
    wide = contract(latent, maps, ((1,), (0,)))
    row = lax.broadcasted_iota(jnp.int32, wide.shape, 0)
    column = lax.broadcasted_iota(jnp.int32, wide.shape, 1)
    wide = jnp.where(row % heads == column // VDIM, wide, 0.0).astype(bf16)
    row = lax.broadcasted_iota(jnp.int32, (reqs, reqs * heads), 0)
    column = lax.broadcasted_iota(jnp.int32, (reqs, reqs * heads), 1)
    gather = (column // heads == row).astype(f32).astype(bf16)
    values = contract(gather, wide, ((1,), (0,))).astype(bf16)
    row = lax.broadcasted_iota(jnp.int32, (reqs, width_dev), 0)
    resid = resid_ref[0].astype(f32)
    spread = jnp.where(row % 2 == 0, resid[0:1], resid[1:2])
    spread = jnp.where(row // 2 == lax.axis_index("section"), spread, 0.0)
    head = lax.axis_index("head")
    for k in range(n_head):
        columns = slice(k * width_dev, (k + 1) * width_dev)
        term = contract(values, out_w_ref[:, columns], ((1,), (0,)))
        term = (term + jnp.where(head == k, spread, 0.0)).astype(bf16)
        for s in range(n_section):
            term_ref[s, k] = term


def rows_kernel(terms_ref, hidden_ref):
    reqs, width_dev = hidden_ref.shape
    terms = terms_ref[...].astype(f32).reshape(-1, reqs, width_dev)
    hidden_ref[...] = jnp.sum(terms, axis=0).astype(bf16)


def weigh_kernel(hidden_ref, picks_ref, logits_ref, weight_ref, mine_ref):
    rows_dev, n_expert = weight_ref.shape
    affinity = jax.nn.sigmoid(logits_ref[0])
    share = route_scale * affinity / jnp.sum(affinity, axis=1, keepdims=True)
    expert = lax.broadcasted_iota(jnp.int32, (rows_dev, n_expert), 1)
    weight = jnp.zeros((rows_dev, n_expert), f32)
    picks = picks_ref[0]
    for k in range(picks.shape[1]):
        weight += jnp.where(picks[:, k : k + 1] == expert, share[:, k : k + 1], 0.0)
    weight_ref[...] = weight
    hidden = hidden_ref[...].astype(f32)
    section = lax.axis_index("section")
    total = jnp.zeros(mine_ref.shape, f32)
    for s in range(hidden.shape[0] // rows_dev):
        total += jnp.where(section == s, hidden[s * rows_dev : (s + 1) * rows_dev], 0.0)
    mine_ref[...] = total


def expert_in_kernel(r0, r1, r2, r3, gate_ref, up_ref, after_ref, both_ref):
    wide = jnp.concatenate([r[...].astype(f32) for r in (r0, r1, r2, r3)], axis=0)
    rows = wide.astype(bf16)
    squares = jnp.sum(wide * wide, axis=1, keepdims=True)
    squares = jnp.sum(jnp.where(diagonal(rows.shape[0]), squares, 0.0), axis=0, keepdims=True)
    high = squares.astype(bf16).astype(f32)
    middle = (squares - high).astype(bf16).astype(f32)
    row = lax.broadcasted_iota(jnp.int32, (8, 128), 0)
    low = jnp.where(row == 2, squares - high - middle, 0.0)
    squares = jnp.where(row == 0, high, jnp.where(row == 1, middle, low))
    n_head = both_ref.shape[0]
    ff = gate_ref.shape[2] // n_head
    for k in range(n_head):
        columns = slice(k * ff, (k + 1) * ff)
        parts = []
        for w in (gate_ref, up_ref):
            sums = contract(rows, w[0, :, columns], ((1,), (0,)))
            parts += [sums[:, c : c + 128] for c in range(0, ff, 128)]
        both_ref[k] = jnp.concatenate(parts + [squares], axis=0).astype(bf16)


def diagonal(rows):
    row = lax.broadcasted_iota(jnp.int32, (rows, 128), 0)
    return row == lax.broadcasted_iota(jnp.int32, (rows, 128), 1)


def act_kernel(both_ref, act_ref):
    both = jnp.sum(both_ref[...].astype(f32), axis=0)
    count, ff = act_ref.shape[1:]
    blocks = [both[i * count : (i + 1) * count] for i in range(2 * ff // 128)]
    squares = jnp.sum(both[2 * ff // 128 * count :], axis=0, keepdims=True)
    squares = jnp.sum(jnp.where(diagonal(count), squares, 0.0), axis=1, keepdims=True)
    factor = lax.rsqrt(squares / D + norm_eps)
    gate = jnp.concatenate(blocks[: ff // 128], axis=1) * factor
    up = jnp.concatenate(blocks[ff // 128 :], axis=1) * factor
    act = (gate * jax.nn.sigmoid(gate) * up).astype(bf16)
    for k in range(act_ref.shape[0]):
        act_ref[k] = act


def expert_out_kernel(n_section, n_group, act_ref, down_ref, served_ref):
    n_head, _, ff = act_ref.shape
    act = jnp.concatenate([act_ref[k] for k in range(n_head)], axis=1)
    total = contract(act, down_ref[0], ((1,), (0,)))
    group = lax.axis_index("group")
    rows_dev = served_ref.shape[1]
    for d in range(n_group):
        for s in range(n_section):
            start = (d * n_section + s) * rows_dev
            served_ref[s * n_group + (group ^ d)] = total[start : start + rows_dev].astype(bf16)


def finish_kernel(back_ref, weight_ref, mine_ref, out_ref):
    weight = weight_ref[...]
    total = mine_ref[...]
    for e in range(back_ref.shape[0]):
        total += weight[:, e : e + 1] * back_ref[e].astype(f32)
    out_ref[0] = total.astype(bf16)


def run(kernel, shapes, *args, far=(), scratch=(), limit=16):
    single = isinstance(shapes[0], int)
    args = [
        pltpu.with_memory_space_constraint(a, pltpu.HBM) if i in far else a
        for i, a in enumerate(args)
    ]
    shapes = [
        jax.ShapeDtypeStruct(shape, bf16) if isinstance(shape, tuple) else shape
        for shape in ([shapes] if single else shapes)
    ]
    return pl.pallas_call(
        kernel,
        out_shape=shapes[0] if single else shapes,
        in_specs=[FAR if i in far else VMEM for i in range(len(args))],
        out_specs=VMEM if single else [VMEM] * len(shapes),
        scratch_shapes=list(scratch),
        compiler_params=pltpu.CompilerParams(vmem_limit_bytes=limit * 1024 * 1024),
    )(*args)


def local(
    queries, cache, kept_length, w_uv, w_out, resid, picks, pick_logits, w_gate, w_up, w_down
):
    n_section = lax.axis_size("section")
    n_group = lax.axis_size("group")
    n_head = lax.axis_size("head")
    n_shard = n_section * n_head
    n_expert = n_section * n_group
    reqs, heads_dev, width = queries.shape[1:]
    rows_dev, width_dev = resid.shape[1:]

    block = cache.shape[2]
    pages = jnp.swapaxes(cache[0], 1, 2).reshape(4, 2, width, block)
    dma = pltpu.SemaphoreType.DMA

    def passed(part, ds, dz):
        pairs = [
            (
                s * n_head + h,
                (s + ds) % n_section * n_head + (h + 2 * dz) % n_head,
            )
            for s in range(n_section)
            for h in range(n_head)
        ]
        return lax.ppermute(part, SPLIT, pairs)

    asked, own, *parts, lengths = run(
        functools.partial(prepare_kernel, n_section, n_head),
        [(n_shard, 2 * heads_dev, width)]
        + [(2, width, block)] * 4
        + [jax.ShapeDtypeStruct(kept_length.shape, jnp.int32)],
        queries,
        pages,
        kept_length,
        far=(0, 1, 2),
        scratch=[pltpu.VMEM((reqs, heads_dev, width), bf16), dma(()), dma((5,))],
    )
    moved = [passed(part, *way) for part, way in zip(parts, ((1, 0), (0, 1), (-1, -1)))]
    q_all = exchange(asked.reshape(n_shard * 2 * heads_dev, width), SPLIT)
    sent = run(
        functools.partial(attend_kernel, n_section, n_head),
        (q_all.shape[0], LAT + 128),
        q_all,
        lengths,
        own,
        *moved,
        w_out,
        far=(6,),
    )
    got = exchange(sent, SPLIT)
    term = run(
        functools.partial(project_kernel, n_section, n_head),
        (n_section, n_head, reqs, width_dev),
        got,
        w_uv,
        w_out,
        resid,
        w_gate,
        w_up,
        far=(4, 5),
    )
    terms = exchange(term.reshape(n_shard * reqs, width_dev), SPLIT)
    hidden = run(rows_kernel, (reqs, width_dev), terms)

    def from_group(d):
        return lax.ppermute(hidden, "group", [(g, g ^ d) for g in range(n_group)])

    others = [from_group(d) for d in range(1, n_group)]

    weight, mine = run(
        weigh_kernel,
        [
            jax.ShapeDtypeStruct((rows_dev, n_expert), f32),
            jax.ShapeDtypeStruct((rows_dev, width_dev), f32),
        ],
        hidden,
        picks,
        pick_logits,
    )

    ff_dev = w_gate.shape[2] // n_head
    count = n_group * reqs
    both = run(
        expert_in_kernel,
        (n_head, 2 * ff_dev // 128 * count + 8, 128),
        hidden,
        *others,
        w_gate,
        w_up,
        mine,
    )
    both = exchange(both, "head")
    act = run(act_kernel, (n_head, count, ff_dev), both)
    act = exchange(act, "head")
    served = run(
        functools.partial(expert_out_kernel, n_section, n_group),
        (n_expert, rows_dev, width_dev),
        act,
        w_down,
    )
    back = exchange(served, ("section", "group"))
    return run(finish_kernel, (1, rows_dev, width_dev), back, weight, mine)


def solution(mesh):
    return jax.shard_map(
        local,
        mesh=mesh,
        in_specs=(
            P("group", None, ("section", "head"), None),
            P("group", None, ("section", "head"), None),
            P("group", None),
            P(("section", "head"), None, None),
            P(("section", "head"), None),
            P("group", "section", "head"),
            P("group", "section", None),
            P("group", "section", None),
            P(("section", "group"), "head", None),
            P(("section", "group"), "head", None),
            P(("section", "group"), None, "head"),
        ),
        out_specs=P("group", "section", "head"),
        check_vma=False,
    )
```

```python
import functools

import jax
import jax.numpy as jnp
from jax import lax
from jax.experimental import pallas as pl
from jax.experimental.pallas import tpu as pltpu
from jax.sharding import PartitionSpec as P

LAT = 512
ROPE = 64
VDIM = 128
D = 7168

neg_fill = -1e30
norm_eps = 1e-06
route_scale = 2.5
f32 = jnp.float32
bf16 = jnp.bfloat16
SPLIT = ("section", "head")
VMEM = pl.BlockSpec(memory_space=pltpu.VMEM)
FAR = pl.BlockSpec(memory_space=pltpu.HBM)


def exchange(x, axes):
    return lax.all_to_all(x, axes, split_axis=0, concat_axis=0, tiled=True)


def contract(a, b, dims):
    return lax.dot_general(a, b, (dims, ((), ())), preferred_element_type=f32)


def in_lanes(x):
    high = x.astype(bf16).astype(f32)
    rest = x - high
    middle = rest.astype(bf16).astype(f32)
    lane = lax.broadcasted_iota(jnp.int32, (x.shape[0], 128), 1)
    zero = jnp.zeros((x.shape[0], 128), f32)
    low = jnp.where(lane == 2, rest - middle, zero)
    return jnp.where(lane == 0, high, jnp.where(lane == 1, middle, low))


def start_all(moves):
    for move in moves:
        move.start()


def wait_all(moves):
    for move in moves:
        move.wait()


def label_here():
    return 2 * (lax.axis_index("section") % 2) + (lax.axis_index("head") // 2) % 2


def prepare_kernel(
    n_section,
    n_head,
    queries_ref,
    cache_ref,
    length_ref,
    asked_ref,
    p0,
    p1,
    p2,
    p3,
    length,
    q,
    q_sem,
    sems,
):
    label = label_here()
    asked = pltpu.make_async_copy(queries_ref.at[0], q, q_sem)
    asked.start()
    moves = [
        pltpu.make_async_copy(cache_ref.at[label ^ d], p, sems.at[i])
        for i, (d, p) in enumerate(((2, p1), (1, p2), (3, p3), (0, p0)))
    ]
    moves.append(pltpu.make_async_copy(length_ref, length, sems.at[4]))
    start_all(moves)
    asked.wait()
    heads = q.shape[1]
    for which in range(4):
        rows = [q[2 * which + r].astype(f32) for r in range(2)]
        block = jnp.concatenate(rows, axis=0).astype(bf16)
        for s in range(which // 2, n_section, 2):
            for z in range(which % 2, n_head // 2, 2):
                for y in range(2):
                    asked_ref[s * n_head + 2 * z + y] = block
    wait_all(moves)


def attend_kernel(
    n_section,
    n_head,
    q_ref,
    length_ref,
    k0,
    k1,
    k2,
    k3,
    ahead_ref,
    out_ref,
):
    section = lax.axis_index("section")
    head = lax.axis_index("head")
    label = label_here()
    block = k0.shape[2]
    sources = (
        (section, head),
        ((section + n_section - 1) % n_section, head),
        (section, (head + n_head - 2) % n_head),
        ((section + 1) % n_section, (head + 2) % n_head),
    )
    lane = lax.broadcasted_iota(jnp.int32, (1, block), 1)
    position = jnp.concatenate([(s * n_head + h) * block + lane for s, h in sources], axis=1)
    length = length_ref[...]
    named = lax.broadcasted_iota(jnp.int32, length.shape, 1) - 2 * label
    asked = q_ref[...].astype(f32).reshape(-1, 2, 8, q_ref.shape[1])
    asked = by_half(asked[:, 0], asked[:, 1])
    outs = []
    for r in range(2):
        page = jnp.concatenate([k[r] for k in (k0, k1, k2, k3)], axis=1)
        q = asked[r].reshape(-1, q_ref.shape[1]).astype(bf16)
        scores = contract(q, page, ((1,), (0,))) * ((VDIM + ROPE) ** -0.5)
        limit = jnp.sum(jnp.where(named == r, length, 0), axis=1, keepdims=True)
        counted = position < limit
        top = jnp.max(jnp.where(counted, scores, neg_fill), axis=1, keepdims=True)
        weights = jnp.where(counted, jnp.exp(scores - top), 0.0)
        total = jnp.sum(weights, axis=1, keepdims=True)
        out = contract(weights.astype(bf16), page[:LAT], ((1,), (1,)))
        any_kept = total > 0
        safe = jnp.where(any_kept, total, 1.0)
        level = in_lanes(jnp.where(any_kept, top + jnp.log(safe), neg_fill))
        outs.append(jnp.concatenate([out / safe, level], axis=1).reshape(-1, 8, LAT + 128))
    sent = jnp.stack(by_half(*outs), axis=1)
    out_ref[...] = sent.reshape(out_ref.shape).astype(bf16)


def by_half(first, second):
    upper = lax.broadcasted_iota(jnp.int32, first.shape, 1) < 4
    return (
        jnp.where(upper, first, pltpu.roll(second, 4, axis=1)),
        jnp.where(upper, pltpu.roll(first, 4, axis=1), second),
    )


def project_kernel(
    n_section, n_head, got_ref, uv_ref, out_w_ref, resid_ref, ahead_gate, ahead_up, term_ref
):
    reqs, width_dev = term_ref.shape[2:]
    got = got_ref[...].astype(f32).reshape(n_section * n_head, 8, LAT + 128)
    level = jnp.sum(got[:, :, LAT:], axis=2, keepdims=True)
    merged = []
    for label in range(4):
        parts = [
            (2 * a + label // 2) * n_head + 2 * (2 * b + label % 2) + c
            for a in range(n_section // 2)
            for b in range(n_head // 4)
            for c in range(2)
        ]
        top = functools.reduce(jnp.maximum, [level[d] for d in parts])
        share = [jnp.exp(level[d] - top) for d in parts]
        total = functools.reduce(jnp.add, share)
        mix = functools.reduce(jnp.add, [w * got[d, :, :LAT] for w, d in zip(share, parts)])
        merged.append(mix / total)
    latent = jnp.concatenate(merged, axis=0).astype(bf16)
    heads = uv_ref.shape[0]
    maps = jnp.concatenate([uv_ref[i] for i in range(heads)], axis=1)
    wide = contract(latent, maps, ((1,), (0,)))
    row = lax.broadcasted_iota(jnp.int32, wide.shape, 0)
    column = lax.broadcasted_iota(jnp.int32, wide.shape, 1)
    wide = jnp.where(row % heads == column // VDIM, wide, 0.0).astype(bf16)
    row = lax.broadcasted_iota(jnp.int32, (reqs, reqs * heads), 0)
    column = lax.broadcasted_iota(jnp.int32, (reqs, reqs * heads), 1)
    gather = (column // heads == row).astype(f32).astype(bf16)
    values = contract(gather, wide, ((1,), (0,))).astype(bf16)
    row = lax.broadcasted_iota(jnp.int32, (reqs, width_dev), 0)
    resid = resid_ref[0].astype(f32)
    spread = jnp.where(row % 2 == 0, resid[0:1], resid[1:2])
    spread = jnp.where(row // 2 == lax.axis_index("section"), spread, 0.0)
    head = lax.axis_index("head")
    for k in range(0, n_head, 2):
        columns = slice(k * width_dev, (k + 2) * width_dev)
        pair = contract(values, out_w_ref[:, columns], ((1,), (0,)))
        for d in range(2):
            term = pair[:, d * width_dev : (d + 1) * width_dev]
            term = (term + jnp.where(head == k + d, spread, 0.0)).astype(bf16)
            for s in range(n_section):
                term_ref[s, k + d] = term


def rows_kernel(terms_ref, hidden_ref):
    reqs, width_dev = hidden_ref.shape
    terms = terms_ref[...].astype(f32).reshape(-1, reqs, width_dev)
    hidden_ref[...] = jnp.sum(terms, axis=0).astype(bf16)


def weigh_kernel(hidden_ref, picks_ref, logits_ref, weight_ref, mine_ref):
    rows_dev, n_expert = weight_ref.shape
    affinity = jax.nn.sigmoid(logits_ref[0])
    share = route_scale * affinity / jnp.sum(affinity, axis=1, keepdims=True)
    expert = lax.broadcasted_iota(jnp.int32, (rows_dev, n_expert), 1)
    weight = jnp.zeros((rows_dev, n_expert), f32)
    picks = picks_ref[0]
    for k in range(picks.shape[1]):
        weight += jnp.where(picks[:, k : k + 1] == expert, share[:, k : k + 1], 0.0)
    weight_ref[...] = weight
    hidden = hidden_ref[...].astype(f32)
    section = lax.axis_index("section")
    total = jnp.zeros(mine_ref.shape, f32)
    for s in range(hidden.shape[0] // rows_dev):
        total += jnp.where(section == s, hidden[s * rows_dev : (s + 1) * rows_dev], 0.0)
    mine_ref[...] = total


def expert_in_kernel(r0, r1, r2, r3, gate_ref, up_ref, after_ref, both_ref):
    wide = jnp.concatenate([r[...].astype(f32) for r in (r0, r1, r2, r3)], axis=0)
    rows = wide.astype(bf16)
    squares = jnp.sum(wide * wide, axis=1, keepdims=True)
    squares = jnp.sum(jnp.where(diagonal(rows.shape[0]), squares, 0.0), axis=0, keepdims=True)
    high = squares.astype(bf16).astype(f32)
    middle = (squares - high).astype(bf16).astype(f32)
    row = lax.broadcasted_iota(jnp.int32, (8, 128), 0)
    low = jnp.where(row == 2, squares - high - middle, 0.0)
    squares = jnp.where(row == 0, high, jnp.where(row == 1, middle, low))
    n_head = both_ref.shape[0]
    ff = gate_ref.shape[2] // n_head
    for k in range(n_head):
        columns = slice(k * ff, (k + 1) * ff)
        parts = []
        for w in (gate_ref, up_ref):
            sums = contract(rows, w[0, :, columns], ((1,), (0,)))
            parts += [sums[:, c : c + 128] for c in range(0, ff, 128)]
        both_ref[k] = jnp.concatenate(parts + [squares], axis=0).astype(bf16)


def diagonal(rows):
    row = lax.broadcasted_iota(jnp.int32, (rows, 128), 0)
    return row == lax.broadcasted_iota(jnp.int32, (rows, 128), 1)


def act_kernel(both_ref, act_ref):
    both = jnp.sum(both_ref[...].astype(f32), axis=0)
    count, ff = act_ref.shape[1:]
    blocks = [both[i * count : (i + 1) * count] for i in range(2 * ff // 128)]
    squares = jnp.sum(both[2 * ff // 128 * count :], axis=0, keepdims=True)
    squares = jnp.sum(jnp.where(diagonal(count), squares, 0.0), axis=1, keepdims=True)
    factor = lax.rsqrt(squares / D + norm_eps)
    gate = jnp.concatenate(blocks[: ff // 128], axis=1) * factor
    up = jnp.concatenate(blocks[ff // 128 :], axis=1) * factor
    act = (gate * jax.nn.sigmoid(gate) * up).astype(bf16)
    for k in range(act_ref.shape[0]):
        act_ref[k] = act


def expert_out_kernel(n_section, n_group, act_ref, down_ref, served_ref):
    n_head, _, ff = act_ref.shape
    act = jnp.concatenate([act_ref[k] for k in range(n_head)], axis=1)
    total = contract(act, down_ref[0], ((1,), (0,)))
    group = lax.axis_index("group")
    rows_dev = served_ref.shape[1]
    for d in range(n_group):
        for s in range(n_section):
            start = (d * n_section + s) * rows_dev
            served_ref[s * n_group + (group ^ d)] = total[start : start + rows_dev].astype(bf16)


def finish_kernel(back_ref, weight_ref, mine_ref, out_ref):
    weight = weight_ref[...]
    total = mine_ref[...]
    for e in range(back_ref.shape[0]):
        total += weight[:, e : e + 1] * back_ref[e].astype(f32)
    out_ref[0] = total.astype(bf16)


def run(kernel, shapes, *args, far=(), scratch=(), limit=16):
    single = isinstance(shapes[0], int)
    args = [
        pltpu.with_memory_space_constraint(a, pltpu.HBM) if i in far else a
        for i, a in enumerate(args)
    ]
    shapes = [
        jax.ShapeDtypeStruct(shape, bf16) if isinstance(shape, tuple) else shape
        for shape in ([shapes] if single else shapes)
    ]
    return pl.pallas_call(
        kernel,
        out_shape=shapes[0] if single else shapes,
        in_specs=[FAR if i in far else VMEM for i in range(len(args))],
        out_specs=VMEM if single else [VMEM] * len(shapes),
        scratch_shapes=list(scratch),
        compiler_params=pltpu.CompilerParams(vmem_limit_bytes=limit * 1024 * 1024),
    )(*args)


def local(
    queries, cache, kept_length, w_uv, w_out, resid, picks, pick_logits, w_gate, w_up, w_down
):
    n_section = lax.axis_size("section")
    n_group = lax.axis_size("group")
    n_head = lax.axis_size("head")
    n_shard = n_section * n_head
    n_expert = n_section * n_group
    reqs, heads_dev, width = queries.shape[1:]
    rows_dev, width_dev = resid.shape[1:]

    block = cache.shape[2]
    pages = jnp.swapaxes(cache[0], 1, 2).reshape(4, 2, width, block)
    dma = pltpu.SemaphoreType.DMA

    def passed(part, ds, dz):
        pairs = [
            (
                s * n_head + h,
                (s + ds) % n_section * n_head + (h + 2 * dz) % n_head,
            )
            for s in range(n_section)
            for h in range(n_head)
        ]
        return lax.ppermute(part, SPLIT, pairs)

    asked, own, *parts, lengths = run(
        functools.partial(prepare_kernel, n_section, n_head),
        [(n_shard, 2 * heads_dev, width)]
        + [(2, width, block)] * 4
        + [jax.ShapeDtypeStruct(kept_length.shape, jnp.int32)],
        queries,
        pages,
        kept_length,
        far=(0, 1, 2),
        scratch=[pltpu.VMEM((reqs, heads_dev, width), bf16), dma(()), dma((5,))],
    )
    moved = [passed(part, *way) for part, way in zip(parts, ((1, 0), (0, 1), (-1, -1)))]
    q_all = exchange(asked.reshape(n_shard * 2 * heads_dev, width), SPLIT)
    sent = run(
        functools.partial(attend_kernel, n_section, n_head),
        (q_all.shape[0], LAT + 128),
        q_all,
        lengths,
        own,
        *moved,
        w_out,
        far=(6,),
    )
    got = exchange(sent, SPLIT)
    term = run(
        functools.partial(project_kernel, n_section, n_head),
        (n_section, n_head, reqs, width_dev),
        got,
        w_uv,
        w_out,
        resid,
        w_gate,
        w_up,
        far=(4, 5),
    )
    terms = exchange(term.reshape(n_shard * reqs, width_dev), SPLIT)
    hidden = run(rows_kernel, (reqs, width_dev), terms)

    def from_group(d):
        return lax.ppermute(hidden, "group", [(g, g ^ d) for g in range(n_group)])

    others = [from_group(d) for d in range(1, n_group)]

    weight, mine = run(
        weigh_kernel,
        [
            jax.ShapeDtypeStruct((rows_dev, n_expert), f32),
            jax.ShapeDtypeStruct((rows_dev, width_dev), f32),
        ],
        hidden,
        picks,
        pick_logits,
    )

    ff_dev = w_gate.shape[2] // n_head
    count = n_group * reqs
    both = run(
        expert_in_kernel,
        (n_head, 2 * ff_dev // 128 * count + 8, 128),
        hidden,
        *others,
        w_gate,
        w_up,
        mine,
    )
    both = exchange(both, "head")
    act = run(act_kernel, (n_head, count, ff_dev), both)
    act = exchange(act, "head")
    served = run(
        functools.partial(expert_out_kernel, n_section, n_group),
        (n_expert, rows_dev, width_dev),
        act,
        w_down,
    )
    back = exchange(served, ("section", "group"))
    return run(finish_kernel, (1, rows_dev, width_dev), back, weight, mine)


def solution(mesh):
    return jax.shard_map(
        local,
        mesh=mesh,
        in_specs=(
            P("group", None, ("section", "head"), None),
            P("group", None, ("section", "head"), None),
            P("group", None),
            P(("section", "head"), None, None),
            P(("section", "head"), None),
            P("group", "section", "head"),
            P("group", "section", None),
            P("group", "section", None),
            P(("section", "group"), "head", None),
            P(("section", "group"), "head", None),
            P(("section", "group"), None, "head"),
        ),
        out_specs=P("group", "section", "head"),
        check_vma=False,
    )
```

```python
import functools

import jax
import jax.numpy as jnp
from jax import lax
from jax.experimental import pallas as pl
from jax.experimental.pallas import tpu as pltpu
from jax.sharding import PartitionSpec as P

LAT = 512
ROPE = 64
VDIM = 128
D = 7168

neg_fill = -1e30
norm_eps = 1e-06
route_scale = 2.5
f32 = jnp.float32
bf16 = jnp.bfloat16
SPLIT = ("section", "head")
VMEM = pl.BlockSpec(memory_space=pltpu.VMEM)
FAR = pl.BlockSpec(memory_space=pltpu.HBM)


def exchange(x, axes):
    return lax.all_to_all(x, axes, split_axis=0, concat_axis=0, tiled=True)


def contract(a, b, dims):
    return lax.dot_general(a, b, (dims, ((), ())), preferred_element_type=f32)


def in_lanes(x):
    high = x.astype(bf16).astype(f32)
    rest = x - high
    middle = rest.astype(bf16).astype(f32)
    lane = lax.broadcasted_iota(jnp.int32, (x.shape[0], 128), 1)
    zero = jnp.zeros((x.shape[0], 128), f32)
    low = jnp.where(lane == 2, rest - middle, zero)
    return jnp.where(lane == 0, high, jnp.where(lane == 1, middle, low))


def start_all(moves):
    for move in moves:
        move.start()


def wait_all(moves):
    for move in moves:
        move.wait()


def label_here():
    return 2 * (lax.axis_index("section") % 2) + (lax.axis_index("head") // 2) % 2


def prepare_kernel(
    n_section,
    n_head,
    queries_ref,
    cache_ref,
    length_ref,
    asked_ref,
    p0,
    p1,
    p2,
    p3,
    length,
    q,
    q_sem,
    sems,
):
    label = label_here()
    asked = pltpu.make_async_copy(queries_ref.at[0], q, q_sem)
    asked.start()
    moves = [
        pltpu.make_async_copy(cache_ref.at[label ^ d], p, sems.at[i])
        for i, (d, p) in enumerate(((2, p1), (1, p2), (3, p3), (0, p0)))
    ]
    moves.append(pltpu.make_async_copy(length_ref, length, sems.at[4]))
    start_all(moves)
    asked.wait()
    heads = q.shape[1]
    for which in range(4):
        rows = [q[2 * which + r].astype(f32) for r in range(2)]
        block = jnp.concatenate(rows, axis=0).astype(bf16)
        for s in range(which // 2, n_section, 2):
            for z in range(which % 2, n_head // 2, 2):
                for y in range(2):
                    asked_ref[s * n_head + 2 * z + y] = block
    wait_all(moves)


def attend_kernel(
    n_section,
    n_head,
    q_ref,
    length_ref,
    k0,
    k1,
    k2,
    k3,
    ahead_ref,
    out_ref,
):
    section = lax.axis_index("section")
    head = lax.axis_index("head")
    label = label_here()
    block = k0.shape[2]
    sources = (
        (section, head),
        ((section + n_section - 1) % n_section, head),
        (section, (head + n_head - 2) % n_head),
        ((section + 1) % n_section, (head + 2) % n_head),
    )
    lane = lax.broadcasted_iota(jnp.int32, (1, block), 1)
    position = jnp.concatenate([(s * n_head + h) * block + lane for s, h in sources], axis=1)
    length = length_ref[...]
    named = lax.broadcasted_iota(jnp.int32, length.shape, 1) - 2 * label
    asked = q_ref[...].astype(f32).reshape(-1, 2, 8, q_ref.shape[1])
    asked = by_half(asked[:, 0], asked[:, 1])
    outs = []
    for r in range(2):
        page = jnp.concatenate([k[r] for k in (k0, k1, k2, k3)], axis=1)
        q = asked[r].reshape(-1, q_ref.shape[1]).astype(bf16)
        scores = contract(q, page, ((1,), (0,))) * ((VDIM + ROPE) ** -0.5)
        limit = jnp.sum(jnp.where(named == r, length, 0), axis=1, keepdims=True)
        counted = position < limit
        top = jnp.max(jnp.where(counted, scores, neg_fill), axis=1, keepdims=True)
        weights = jnp.where(counted, jnp.exp(scores - top), 0.0)
        total = jnp.sum(weights, axis=1, keepdims=True)
        out = contract(weights.astype(bf16), page[:LAT], ((1,), (1,)))
        any_kept = total > 0
        safe = jnp.where(any_kept, total, 1.0)
        level = in_lanes(jnp.where(any_kept, top + jnp.log(safe), neg_fill))
        outs.append(jnp.concatenate([out / safe, level], axis=1).reshape(-1, 8, LAT + 128))
    sent = jnp.stack(by_half(*outs), axis=1)
    out_ref[...] = sent.reshape(out_ref.shape).astype(bf16)


def by_half(first, second):
    upper = lax.broadcasted_iota(jnp.int32, first.shape, 1) < 4
    return (
        jnp.where(upper, first, pltpu.roll(second, 4, axis=1)),
        jnp.where(upper, pltpu.roll(first, 4, axis=1), second),
    )


def project_kernel(
    n_section, n_head, got_ref, uv_ref, out_w_ref, resid_ref, ahead_gate, ahead_up, term_ref
):
    reqs, width_dev = term_ref.shape[2:]
    got = got_ref[...].astype(f32).reshape(n_section * n_head, 8, LAT + 128)
    level = jnp.sum(got[:, :, LAT:], axis=2, keepdims=True)
    merged = []
    for label in range(4):
        parts = [
            (2 * a + label // 2) * n_head + 2 * (2 * b + label % 2) + c
            for a in range(n_section // 2)
            for b in range(n_head // 4)
            for c in range(2)
        ]
        top = functools.reduce(jnp.maximum, [level[d] for d in parts])
        share = [jnp.exp(level[d] - top) for d in parts]
        total = functools.reduce(jnp.add, share)
        mix = functools.reduce(jnp.add, [w * got[d, :, :LAT] for w, d in zip(share, parts)])
        merged.append(mix / total)
    latent = jnp.concatenate(merged, axis=0).astype(bf16)
    heads = uv_ref.shape[0]
    maps = jnp.concatenate([uv_ref[i] for i in range(heads)], axis=1)
    wide = contract(latent, maps, ((1,), (0,)))
    row = lax.broadcasted_iota(jnp.int32, wide.shape, 0)
    column = lax.broadcasted_iota(jnp.int32, wide.shape, 1)
    wide = jnp.where(row % heads == column // VDIM, wide, 0.0).astype(bf16)
    row = lax.broadcasted_iota(jnp.int32, (reqs, reqs * heads), 0)
    column = lax.broadcasted_iota(jnp.int32, (reqs, reqs * heads), 1)
    gather = (column // heads == row).astype(f32).astype(bf16)
    values = contract(gather, wide, ((1,), (0,))).astype(bf16)
    row = lax.broadcasted_iota(jnp.int32, (reqs, width_dev), 0)
    resid = resid_ref[0].astype(f32)
    spread = jnp.where(row % 2 == 0, resid[0:1], resid[1:2])
    spread = jnp.where(row // 2 == lax.axis_index("section"), spread, 0.0)
    head = lax.axis_index("head")
    for k in range(0, n_head, 2):
        columns = slice(k * width_dev, (k + 2) * width_dev)
        pair = contract(values, out_w_ref[:, columns], ((1,), (0,)))
        for d in range(2):
            term = pair[:, d * width_dev : (d + 1) * width_dev]
            term = (term + jnp.where(head == k + d, spread, 0.0)).astype(bf16)
            for s in range(n_section):
                term_ref[s, k + d] = term


def rows_kernel(terms_ref, hidden_ref):
    reqs, width_dev = hidden_ref.shape
    terms = terms_ref[...].astype(f32).reshape(-1, reqs, width_dev)
    hidden_ref[...] = jnp.sum(terms, axis=0).astype(bf16)


def weigh_kernel(hidden_ref, picks_ref, logits_ref, weight_ref, mine_ref):
    rows_dev, n_expert = weight_ref.shape
    affinity = jax.nn.sigmoid(logits_ref[0])
    share = route_scale * affinity / jnp.sum(affinity, axis=1, keepdims=True)
    expert = lax.broadcasted_iota(jnp.int32, (rows_dev, n_expert), 1)
    weight = jnp.zeros((rows_dev, n_expert), f32)
    picks = picks_ref[0]
    for k in range(picks.shape[1]):
        weight += jnp.where(picks[:, k : k + 1] == expert, share[:, k : k + 1], 0.0)
    weight_ref[...] = weight
    hidden = hidden_ref[...].astype(f32)
    section = lax.axis_index("section")
    total = jnp.zeros(mine_ref.shape, f32)
    for s in range(hidden.shape[0] // rows_dev):
        total += jnp.where(section == s, hidden[s * rows_dev : (s + 1) * rows_dev], 0.0)
    mine_ref[...] = total


def expert_in_kernel(r0, r1, r2, r3, gate_ref, up_ref, after_ref, both_ref):
    wide = jnp.concatenate([r[...].astype(f32) for r in (r0, r1, r2, r3)], axis=0)
    rows = wide.astype(bf16)
    squares = jnp.sum(wide * wide, axis=1, keepdims=True)
    squares = jnp.sum(jnp.where(diagonal(rows.shape[0]), squares, 0.0), axis=0, keepdims=True)
    high = squares.astype(bf16).astype(f32)
    middle = (squares - high).astype(bf16).astype(f32)
    row = lax.broadcasted_iota(jnp.int32, (8, 128), 0)
    low = jnp.where(row == 2, squares - high - middle, 0.0)
    squares = jnp.where(row == 0, high, jnp.where(row == 1, middle, low))
    count, cut = rows.shape[0], rows.shape[1] - 128
    none = jnp.zeros((count, 128), f32)
    last = wide[:, cut:]
    tail = jnp.concatenate(
        [
            jnp.concatenate([last, none], axis=1),
            jnp.concatenate([none, last], axis=1),
        ],
        axis=0,
    ).astype(bf16)
    n_head = both_ref.shape[0]
    ff = gate_ref.shape[2] // n_head
    for k in range(n_head):
        columns = slice(k * ff, (k + 1) * ff)
        parts = []
        ends = [w[0, cut:, columns] for w in (gate_ref, up_ref)]
        ends = contract(tail, jnp.concatenate(ends, axis=0), ((1,), (0,)))
        for i, w in enumerate((gate_ref, up_ref)):
            sums = contract(rows[:, :cut], w[0, :cut, columns], ((1,), (0,)))
            sums += ends[i * count : (i + 1) * count]
            parts += [sums[:, c : c + 128] for c in range(0, ff, 128)]
        both_ref[k] = jnp.concatenate(parts + [squares], axis=0).astype(bf16)


def diagonal(rows):
    row = lax.broadcasted_iota(jnp.int32, (rows, 128), 0)
    return row == lax.broadcasted_iota(jnp.int32, (rows, 128), 1)


def act_kernel(both_ref, act_ref):
    both = jnp.sum(both_ref[...].astype(f32), axis=0)
    count, ff = act_ref.shape[1:]
    blocks = [both[i * count : (i + 1) * count] for i in range(2 * ff // 128)]
    squares = jnp.sum(both[2 * ff // 128 * count :], axis=0, keepdims=True)
    squares = jnp.sum(jnp.where(diagonal(count), squares, 0.0), axis=1, keepdims=True)
    factor = lax.rsqrt(squares / D + norm_eps)
    gate = jnp.concatenate(blocks[: ff // 128], axis=1) * factor
    up = jnp.concatenate(blocks[ff // 128 :], axis=1) * factor
    act = (gate * jax.nn.sigmoid(gate) * up).astype(bf16)
    for k in range(act_ref.shape[0]):
        act_ref[k] = act


def expert_out_kernel(n_section, n_group, act_ref, down_ref, served_ref):
    n_head, _, ff = act_ref.shape
    act = jnp.concatenate([act_ref[k] for k in range(n_head)], axis=1)
    total = contract(act, down_ref[0], ((1,), (0,)))
    group = lax.axis_index("group")
    rows_dev = served_ref.shape[1]
    for d in range(n_group):
        for s in range(n_section):
            start = (d * n_section + s) * rows_dev
            served_ref[s * n_group + (group ^ d)] = total[start : start + rows_dev].astype(bf16)


def finish_kernel(back_ref, weight_ref, mine_ref, out_ref):
    weight = weight_ref[...]
    total = mine_ref[...]
    for e in range(back_ref.shape[0]):
        total += weight[:, e : e + 1] * back_ref[e].astype(f32)
    out_ref[0] = total.astype(bf16)


def run(kernel, shapes, *args, far=(), scratch=(), limit=16):
    single = isinstance(shapes[0], int)
    args = [
        pltpu.with_memory_space_constraint(a, pltpu.HBM) if i in far else a
        for i, a in enumerate(args)
    ]
    shapes = [
        jax.ShapeDtypeStruct(shape, bf16) if isinstance(shape, tuple) else shape
        for shape in ([shapes] if single else shapes)
    ]
    return pl.pallas_call(
        kernel,
        out_shape=shapes[0] if single else shapes,
        in_specs=[FAR if i in far else VMEM for i in range(len(args))],
        out_specs=VMEM if single else [VMEM] * len(shapes),
        scratch_shapes=list(scratch),
        compiler_params=pltpu.CompilerParams(vmem_limit_bytes=limit * 1024 * 1024),
    )(*args)


def local(
    queries, cache, kept_length, w_uv, w_out, resid, picks, pick_logits, w_gate, w_up, w_down
):
    n_section = lax.axis_size("section")
    n_group = lax.axis_size("group")
    n_head = lax.axis_size("head")
    n_shard = n_section * n_head
    n_expert = n_section * n_group
    reqs, heads_dev, width = queries.shape[1:]
    rows_dev, width_dev = resid.shape[1:]

    block = cache.shape[2]
    pages = jnp.swapaxes(cache[0], 1, 2).reshape(4, 2, width, block)
    dma = pltpu.SemaphoreType.DMA

    def passed(part, ds, dz):
        pairs = [
            (
                s * n_head + h,
                (s + ds) % n_section * n_head + (h + 2 * dz) % n_head,
            )
            for s in range(n_section)
            for h in range(n_head)
        ]
        return lax.ppermute(part, SPLIT, pairs)

    asked, own, *parts, lengths = run(
        functools.partial(prepare_kernel, n_section, n_head),
        [(n_shard, 2 * heads_dev, width)]
        + [(2, width, block)] * 4
        + [jax.ShapeDtypeStruct(kept_length.shape, jnp.int32)],
        queries,
        pages,
        kept_length,
        far=(0, 1, 2),
        scratch=[pltpu.VMEM((reqs, heads_dev, width), bf16), dma(()), dma((5,))],
    )
    moved = [passed(part, *way) for part, way in zip(parts, ((1, 0), (0, 1), (-1, -1)))]
    q_all = exchange(asked.reshape(n_shard * 2 * heads_dev, width), SPLIT)
    sent = run(
        functools.partial(attend_kernel, n_section, n_head),
        (q_all.shape[0], LAT + 128),
        q_all,
        lengths,
        own,
        *moved,
        w_out,
        far=(6,),
    )
    got = exchange(sent, SPLIT)
    term = run(
        functools.partial(project_kernel, n_section, n_head),
        (n_section, n_head, reqs, width_dev),
        got,
        w_uv,
        w_out,
        resid,
        w_gate,
        w_up,
        far=(4, 5),
    )
    terms = exchange(term.reshape(n_shard * reqs, width_dev), SPLIT)
    hidden = run(rows_kernel, (reqs, width_dev), terms)

    def from_group(d):
        return lax.ppermute(hidden, "group", [(g, g ^ d) for g in range(n_group)])

    others = [from_group(d) for d in range(1, n_group)]

    weight, mine = run(
        weigh_kernel,
        [
            jax.ShapeDtypeStruct((rows_dev, n_expert), f32),
            jax.ShapeDtypeStruct((rows_dev, width_dev), f32),
        ],
        hidden,
        picks,
        pick_logits,
    )

    ff_dev = w_gate.shape[2] // n_head
    count = n_group * reqs
    both = run(
        expert_in_kernel,
        (n_head, 2 * ff_dev // 128 * count + 8, 128),
        hidden,
        *others,
        w_gate,
        w_up,
        mine,
    )
    both = exchange(both, "head")
    act = run(act_kernel, (n_head, count, ff_dev), both)
    act = exchange(act, "head")
    served = run(
        functools.partial(expert_out_kernel, n_section, n_group),
        (n_expert, rows_dev, width_dev),
        act,
        w_down,
    )
    back = exchange(served, ("section", "group"))
    return run(finish_kernel, (1, rows_dev, width_dev), back, weight, mine)


def solution(mesh):
    return jax.shard_map(
        local,
        mesh=mesh,
        in_specs=(
            P("group", None, ("section", "head"), None),
            P("group", None, ("section", "head"), None),
            P("group", None),
            P(("section", "head"), None, None),
            P(("section", "head"), None),
            P("group", "section", "head"),
            P("group", "section", None),
            P("group", "section", None),
            P(("section", "group"), "head", None),
            P(("section", "group"), "head", None),
            P(("section", "group"), None, "head"),
        ),
        out_specs=P("group", "section", "head"),
        check_vma=False,
    )
```
